128 devices in a mesh: seq: 16 (over y_lo, x, core), dp: 8 (over z, y_hi).
Axes of the slice: x: 4, y: 4 (y_hi: 2, y_lo: 2; y = y_hi * 2 + y_lo), z: 4, core: 2. Of those that a mesh axis runs over, the one named last changes fastest.
Arguments:
- hidden: bfloat16 [8, 2048, 2048], P('dp', 'seq'), may hold values from -6 to 6
- short_taps: bfloat16 [4, 2048], replicated, may hold values from -3 to 3
- long_taps: bfloat16 [256, 16], replicated, may hold values from -0.375 to 0.375
- gate_weight: bfloat16 [2048, 2048], replicated, may hold values from -0.125 to 0.125
- upstream: bfloat16 [8, 2048, 2048], P('dp', 'seq'), may hold values from -6 to 6
Outputs:
- mixed_out: bfloat16 [8, 2048, 2048], P('dp', 'seq')
- grad_gate: float32 [2048, 2048], P(('seq', 'dp'))
- grad_short: float32 [4, 2048], replicated
- grad_long: float32 [256, 16], replicated
- d_hidden: bfloat16 [8, 2048, 2048], P('dp', 'seq')
The draws below stay inside these ranges and needn't reach their ends.
All inputs are finite; a program needn't handle non-finite values.
Results may differ from the reference program's by a relative error of at most 0.0065.
Values may be sent and summed in bfloat16 or wider, within the bound.
A program may use at most 128 MiB of HBM per device.

```python
import jax
import jax.numpy as jnp
from jax import lax

D = 2048
G = 16
KS = 4
KL = 256
L = 2048
B = 8


def block_levels(rng, dims, pieces, low, largest):
    loudness = 1.0
    for axis_at, shards_of in pieces:
        draws = jax.random.uniform(jax.random.fold_in(jax.random.fold_in(rng, 6), axis_at), (shards_of,), jnp.float32, low / len(pieces), largest / len(pieces))
        loudness = loudness * jnp.repeat(jnp.exp(draws), dims[axis_at] // shards_of).reshape((-1,) + (1,) * (len(dims) - 1 - axis_at))
    return loudness


def scatter_about(own_key, shape, width, reach, shards=(), kind=jnp.bfloat16):
    array = jax.random.normal(own_key, shape, jnp.float32) * width
    if len(shards) > 0:
        array = block_levels(own_key, shape, shards, -0.22, 0.18) * array
    return jnp.clip(array, min=-reach, max=reach).astype(kind)


def setup_inputs(seed: int = 0) -> dict:
    key_of = jax.random.split(jax.random.key(seed), 6)
    return {
        "hidden": scatter_about(key_of[0], (B, L, D), 1.0, 6.0, ((0, 8), (1, 16))),
        "short_taps": scatter_about(key_of[1], (KS, D), KS ** -0.5, 3.0),
        "long_taps": scatter_about(key_of[2], (KL, G), KL ** -0.5, 0.375),
        "gate_weight": scatter_about(key_of[3], (D, D), D ** -0.5, 0.125),
        "upstream": scatter_about(key_of[4], (B, L, D), 1.0, 6.0, ((0, 8), (1, 16))),
    }


def causal_filter(signal, filters):
    length = signal.shape[0]
    fft_size = length + filters.shape[0]
    spectrum = jnp.fft.rfft(signal, n=fft_size, axis=0) * jnp.fft.rfft(filters, n=fft_size, axis=0)
    return jnp.fft.irfft(spectrum, n=fft_size, axis=0)[:length]


def lag_products(grads_in, inputs_in, lag_count):
    fft_size = grads_in.shape[0] + lag_count
    spectrum = jnp.fft.rfft(grads_in, n=fft_size, axis=0) * jnp.conj(jnp.fft.rfft(inputs_in, n=fft_size, axis=0))
    return jnp.fft.irfft(spectrum, n=fft_size, axis=0)[:lag_count]


def strand_pass(strand_in, d_gated, short_taps, long_taps, gate_weight):
    length = strand_in.shape[0]
    filters = jnp.repeat(long_taps.astype(jnp.float32), D // G, axis=1)
    x_padded = jnp.pad(strand_in.astype(jnp.float32), ((KS - 1, 0), (0, 0)))
    short_sum = jnp.zeros((length, D), jnp.float32)
    for tap_index in range(KS):
        start_row = KS - 1 - tap_index
        short_sum = short_sum + short_taps[tap_index].astype(jnp.float32) * x_padded[start_row:start_row + length]
    short_out = short_sum.astype(jnp.bfloat16)
    long_out = causal_filter(short_out.astype(jnp.float32), filters)
    gate_pre = jnp.dot(strand_in, gate_weight, preferred_element_type=jnp.float32)
    sigmoid_gate = jax.nn.sigmoid(gate_pre)
    gated = (gate_pre * sigmoid_gate * long_out).astype(jnp.bfloat16)
    d_float = d_gated.astype(jnp.float32)
    d_long = (d_float * gate_pre * sigmoid_gate).astype(jnp.bfloat16)
    d_gate = (d_float * long_out * sigmoid_gate * (1.0 + gate_pre * (1.0 - sigmoid_gate))).astype(jnp.bfloat16)
    gate_term = jnp.dot(strand_in.T, d_gate, preferred_element_type=jnp.float32)
    d_short = jnp.flip(causal_filter(jnp.flip(d_long.astype(jnp.float32), 0), filters), 0).astype(jnp.bfloat16)
    lag_term = lag_products(d_long.astype(jnp.float32), short_out.astype(jnp.float32), KL)
    lag_term = jnp.sum(lag_term.reshape(KL, G, D // G), axis=2)
    d_short_f = d_short.astype(jnp.float32)
    d_padded = jnp.pad(d_short_f, ((0, KS - 1), (0, 0)))
    dx_short = jnp.zeros((length, D), jnp.float32)
    short_rows = []
    for tap_index in range(KS):
        dx_short = dx_short + short_taps[tap_index].astype(jnp.float32) * d_padded[tap_index:tap_index + length]
        start_row = KS - 1 - tap_index
        short_rows.append(jnp.sum(d_short_f * x_padded[start_row:start_row + length], axis=0))
    short_term = jnp.stack(short_rows)
    d_input = (jnp.dot(d_gate, gate_weight.T, preferred_element_type=jnp.float32) + dx_short).astype(jnp.bfloat16)
    return gated, gate_term, short_term, lag_term, d_input


def reference(hidden, short_taps, long_taps, gate_weight, upstream):
    def one_sequence(carry, inputs):
        seq_in, cotangent = inputs
        forward_parts = strand_pass(seq_in, cotangent, short_taps, long_taps, gate_weight)
        reverse_parts = strand_pass(jnp.flip(seq_in, (0, 1)), jnp.flip(cotangent, (0, 1)), short_taps, long_taps, gate_weight)
        mixed_row = (forward_parts[0].astype(jnp.float32) + jnp.flip(reverse_parts[0], (0, 1)).astype(jnp.float32)).astype(jnp.bfloat16)
        grad_row = (forward_parts[4].astype(jnp.float32) + jnp.flip(reverse_parts[4], (0, 1)).astype(jnp.float32)).astype(jnp.bfloat16)
        new_carry = tuple(held + first_term + second_term for held, first_term, second_term in zip(carry, forward_parts[1:4], reverse_parts[1:4]))
        return new_carry, (mixed_row, grad_row)

    initial = (jnp.zeros((D, D), jnp.float32), jnp.zeros((KS, D), jnp.float32), jnp.zeros((KL, G), jnp.float32))
    totals, outputs = lax.scan(one_sequence, initial, (hidden, upstream))
    return outputs[0], totals[0], totals[1], totals[2], outputs[1]
```

```python
import types

import jax
import jax.numpy as jnp
from jax import lax
from jax.experimental import pallas as pl
from jax.experimental.pallas import tpu as pltpu
from jax.sharding import PartitionSpec as P

BF = jnp.bfloat16
F32 = jnp.float32
MESH = pl.DeviceIdType.MESH
NT = (((1,), (1,)), ((), ()))
TN = (((0,), (0,)), ((), ()))

WIDTHS = (256, 384, 384)
STARTS = (0, 256, 640)
RING = 4
SMALL = 1280

SCRATCH = dict(
    hh=((512, 2048), BF),
    w=((2048, 1024), BF),
    up=((256, 1024), BF),
    upj=((256, 1024), BF),
    halo=((2, 16, 2048), BF),
    st=((4, 2048), F32),
    xf=((272, 1024), BF),
    xr=((272, 1024), BF),
    sf=((512, 1024), BF),
    sr=((512, 1024), BF),
    df=((512, 1024), BF),
    dr=((512, 1024), BF),
    gate=((512, 1024), F32),
    gr=((512, 1024), BF),
    mx=((256, 1024), BF),
    dg=((512, 1024), BF),
    tt=((8, 256, 512), BF),
    uu=((8, 256, 512), BF),
    tv=((16, 512), F32),
    uv=((16, 512), F32),
    jm=((256, 256), BF),
    im=((256, 256), BF),
    xt=((2048, 512), BF),
    pa=((2, 4, 256, WIDTHS[0]), BF),
    pb=((2, 32, 2, 16, WIDTHS[1]), BF),
    pc=((16, 4, 32, WIDTHS[2]), BF),
    ra1=((3, 2, 256, WIDTHS[0]), BF),
    rb1=((3, 32, 16, WIDTHS[1]), BF),
    rc1=((3, 16, 32, WIDTHS[2]), BF),
    sa1=((2, 8, 2, 16, WIDTHS[0]), BF),
    sb1=((8, 4, 16, WIDTHS[1]), BF),
    sc1=((2, 4, 64, WIDTHS[2]), BF),
    ra2=((3, 8, 16, WIDTHS[0]), BF),
    rb2=((3, 8, 16, WIDTHS[1]), BF),
    rc2=((3, 2, 64, WIDTHS[2]), BF),
    sa2=((2, 4, 16, WIDTHS[0]), BF),
    sb2=((4, 32, WIDTHS[1]), BF),
    sc2=((2, 2, 2, 16, WIDTHS[2]), BF),
    ra3=((3, 2, 16, WIDTHS[0]), BF),
    rb3=((3, 32, WIDTHS[1]), BF),
    rc3=((3, 2, 16, WIDTHS[2]), BF),
    fin=((2, 16, 1024), F32),
    dsf=((272, 1024), BF),
    dsr=((272, 1024), BF),
    ls=((2, 8, 8, 512), F32),
    sm=((3, 4, 8, SMALL), F32),
    smo=((8, SMALL), F32),
    dh=((256, 2048), F32),
    dxr=((256, 1024), BF),
    dhs=((128, 2048), BF),
    dhr=((128, 2048), BF),
    dho=((128, 2048), BF),
)
LOCAL_SEMS = 16
REMOTE_SEMS = 64


def dot(a, b):
    return jnp.dot(a, b, preferred_element_type=F32)


def dot_nt(a, b):
    return lax.dot_general(a, b, NT, preferred_element_type=F32)


def skew_sum(m, to_left):
    rows, lanes = m.shape
    while rows > 8:
        rows //= 2
        shift = lanes - rows if to_left else rows
        m = m[:rows] + pltpu.roll(m[rows:], shift, 1)
    return m


def kernel(hidden, staps, ltaps, weight, upstream, mixed, ggate, small, dhid, *scratch):
    r = types.SimpleNamespace(**dict(zip(SCRATCH, scratch)))
    loc, send, recv = scratch[len(SCRATCH) :]

    seq, dp = lax.axis_index("seq"), lax.axis_index("dp")
    core = lax.rem(seq, 2)
    chip = seq // 2
    x = lax.rem(chip, 4)
    y_lo = chip // 4
    y_hi = lax.rem(dp, 2)
    y = y_hi * 2 + y_lo
    z = dp // 2
    other = 1 - core

    def at_chip(c, k):
        return {"seq": c * 2 + k, "dp": dp}

    def x_peer(o):
        return {"seq": (y_lo * 4 + lax.rem(x + o, 4)) * 2 + core, "dp": dp}

    def y_peer(o):
        t = lax.rem(y + o, 4)
        return {
            "seq": (lax.rem(t, 2) * 4 + x) * 2 + core,
            "dp": z * 2 + t // 2,
        }

    def z_peer(o):
        return {"seq": seq, "dp": lax.rem(z + o, 4) * 2 + y_hi}

    partner = at_chip(chip, other)
    nxt, prv = lax.rem(chip + 1, 8), lax.rem(chip + 7, 8)
    cross_chip = lax.rem(chip + 8 + 2 * core - 1, 8)
    peers = [partner, at_chip(nxt, core), at_chip(prv, core), at_chip(cross_chip, other)]
    peers += [f(o) for f in (x_peer, y_peer, z_peer) for o in (1, 2, 3)]

    offs = [pl.multiple_of(512 * other, 512), pl.multiple_of(1024 + 512 * core, 512)]
    offs_other = [pl.multiple_of(512 * core, 512), pl.multiple_of(1024 + 512 * other, 512)]
    own = pl.multiple_of(core * 128, 128)
    theirs = pl.multiple_of(other * 128, 128)

    def col(g, width):
        half = 512 // width
        c = jnp.where(g < half, 512 * other + g * width, 512 + 512 * core + g * width)
        return pl.multiple_of(c, width)

    started = []
    count = [0]

    def remote(src, dst, device, recv_index=None):
        i = count[0]
        count[0] += 1
        copy = pltpu.make_async_remote_copy(
            src_ref=src,
            dst_ref=dst,
            send_sem=send.at[i],
            recv_sem=recv.at[i if recv_index is None else recv_index],
            device_id=device,
            device_id_type=MESH,
        )
        copy.start()
        started.append(copy)
        return copy

    lcount = [0]

    def local(src, dst):
        copy = pltpu.make_async_copy(src, dst, loc.at[lcount[0]])
        lcount[0] += 1
        copy.start()
        return copy

    in_h = local(hidden.at[0], r.hh.at[pl.ds(own, 128)])
    in_u = [
        local(
            upstream.at[0, :, pl.ds(offs[i], 512)],
            r.up.at[pl.ds(own, 128), pl.ds(512 * i, 512)],
        )
        for i in range(2)
    ]
    in_w = [
        local(weight.at[:, pl.ds(offs[i], 512)], r.w.at[:, pl.ds(512 * i, 512)])
        for i in range(2)
    ]

    barrier = pltpu.get_barrier_semaphore()
    for peer in peers:
        pl.semaphore_signal(barrier, inc=1, device_id=peer, device_id_type=MESH)
    pl.semaphore_wait(barrier, len(peers))

    halo_base = REMOTE_SEMS - 2
    halo_src = hidden.at[0, pl.ds(pl.multiple_of(core * 112, 16), 16)]
    for k in range(2):
        halo_copy = remote(
            halo_src, r.halo.at[other], at_chip(cross_chip, k), halo_base + other
        )
    pair_h = remote(hidden.at[0], r.hh.at[pl.ds(own, 128)], partner)
    pair_u = [
        remote(
            upstream.at[0, :, pl.ds(offs_other[i], 512)],
            r.up.at[pl.ds(own, 128), pl.ds(512 * i, 512)],
            partner,
        )
        for i in range(2)
    ]

    rows_i = lax.broadcasted_iota(jnp.int32, (256, 256), 0)
    cols_i = lax.broadcasted_iota(jnp.int32, (256, 256), 1)
    r.jm[...] = jnp.where(rows_i + cols_i == 255, 1.0, 0.0).astype(BF)
    r.im[...] = jnp.where(rows_i == cols_i, 1.0, 0.0).astype(BF)
    r.st[...] = staps[...].astype(F32)

    tap_i = lax.broadcasted_iota(jnp.int32, (256, 512), 0)
    lag_i = lax.broadcasted_iota(jnp.int32, (256, 512), 1)
    taps = ltaps[...]
    r.tv[...] = lax.dot_general(
        taps,
        jnp.where(tap_i + lag_i == 256, 1.0, 0.0).astype(BF),
        TN,
        preferred_element_type=F32,
    )
    r.uv[...] = lax.dot_general(
        taps, jnp.where(tap_i == lag_i, 1.0, 0.0).astype(BF), TN, preferred_element_type=F32
    )

    def toeplitz(g, carry):
        gg = col(g, 128) // 128
        for vec, out in ((r.tv, r.tt), (r.uv, r.uu)):
            first = pltpu.roll(
                jnp.broadcast_to(vec[pl.ds(gg, 1), :], (32, 512)), 0, 1, stride=1, stride_axis=0
            )
            for b in range(8):
                block = first if b == 0 else pltpu.roll(first, 32 * b, 1)
                out[g, 32 * b : 32 * b + 32, :] = block.astype(BF)
        return carry

    lax.fori_loop(0, 8, toeplitz, 0)

    in_h.wait()
    pair_h.wait_recv()

    def flip_rows(i, carry):
        here = pl.multiple_of(i * 256, 256)
        there = pl.multiple_of(1792 - i * 256, 256)
        r.hh[256:512, pl.ds(here, 256)] = dot(r.hh[0:256, pl.ds(there, 256)], r.jm[...]).astype(BF)
        return carry

    lax.fori_loop(0, 8, flip_rows, 0)

    for k in range(2):
        pltpu.make_async_remote_copy(
            src_ref=halo_src,
            dst_ref=r.halo.at[k],
            send_sem=send.at[0],
            recv_sem=recv.at[halo_base + k],
            device_id=partner,
            device_id_type=MESH,
        ).wait_recv()

    @pl.when(chip == 0)
    def _():
        r.halo[0] = jnp.zeros((16, 2048), BF)

    @pl.when(chip == 7)
    def _():
        r.halo[1] = jnp.zeros((16, 2048), BF)

    for i in range(2):
        span = slice(512 * i, 512 * i + 512)
        r.xf[0:16, span] = r.halo[0, :, pl.ds(offs[i], 512)]
        r.xf[16:272, span] = r.hh[0:256, pl.ds(offs[i], 512)]
        r.xr[0:256, span] = r.hh[256:512, pl.ds(offs[i], 512)]
    for i in range(4):
        flipped = dot(r.halo[1, :, pl.ds(col(3 - i, 256), 256)], r.jm[...])
        r.xr[256:272, 256 * i : 256 * i + 256] = flipped.astype(BF)

    def short_conv(g, carry):
        here = pl.ds(pl.multiple_of(g * 128, 128), 128)
        there = pl.ds(col(g, 128), 128)
        fwd = r.xf[:, here].astype(F32)
        rev = r.xr[:, here].astype(F32)
        acc_f = r.st[0:1, there] * fwd[16:272]
        acc_r = r.st[0:1, there] * rev[0:256]
        for k in range(1, 4):
            tap = r.st[k : k + 1, there]
            acc_f += tap * pltpu.roll(fwd, k, 0)[16:272]
            acc_r += tap * pltpu.roll(rev, 272 - k, 0)[0:256]
        r.sf[256:512, here] = acc_f.astype(BF)
        r.sr[0:256, here] = acc_r.astype(BF)
        return carry

    lax.fori_loop(0, 8, short_conv, 0)
    rim_sf = remote(r.sf.at[pl.ds(256, 256)], r.sf.at[pl.ds(0, 256)], at_chip(nxt, core))
    rim_sr = remote(r.sr.at[pl.ds(0, 256)], r.sr.at[pl.ds(256, 256)], at_chip(prv, core))

    for copy in in_w + in_u:
        copy.wait()
    for copy in pair_u:
        copy.wait_recv()

    def gate_block(i, carry):
        here = pl.ds(pl.multiple_of(i * 256, 256), 256)
        there = pl.ds(pl.multiple_of(768 - i * 256, 256), 256)
        r.gate[:, here] = dot(r.hh[...], r.w[:, here])
        r.upj[:, here] = dot(r.up[:, there], r.jm[...]).astype(BF)

        def rows(b, carry):
            at = pl.multiple_of(b * 32, 32)
            gf = r.gate[pl.ds(at, 32), here]
            gb = r.gate[pl.ds(at + 256, 32), here]
            uf = r.up[pl.ds(at, 32), here].astype(F32)
            ub = r.upj[pl.ds(at, 32), here].astype(F32)
            r.df[pl.ds(at, 32), here] = (uf * gf * jax.nn.sigmoid(gf)).astype(BF)
            r.dr[pl.ds(at + 256, 32), here] = (ub * gb * jax.nn.sigmoid(gb)).astype(BF)
            return carry

        return lax.fori_loop(0, 8, rows, carry)

    lax.fori_loop(0, 4, gate_block, 0)
    rim_df = remote(r.df.at[pl.ds(0, 256)], r.df.at[pl.ds(256, 256)], at_chip(prv, core))
    rim_dr = remote(r.dr.at[pl.ds(256, 256)], r.dr.at[pl.ds(0, 256)], at_chip(nxt, core))

    def transposed(i, carry):
        here = pl.ds(pl.multiple_of(i * 256, 256), 256)
        r.xt[here, 0:256] = dot_nt(r.im[...], r.hh[0:256, here]).astype(BF)
        r.xt[here, 256:512] = dot_nt(r.im[...], r.hh[256:512, here]).astype(BF)
        return carry

    lax.fori_loop(0, 8, transposed, 0)

    rim_sf.wait_recv()
    rim_sr.wait_recv()

    @pl.when(chip == 0)
    def _():
        r.sf[0:256, :] = jnp.zeros((256, 1024), BF)

    @pl.when(chip == 7)
    def _():
        r.sr[256:512, :] = jnp.zeros((256, 1024), BF)

    def long_conv(g, carry):
        here = pl.ds(pl.multiple_of(g * 128, 128), 128)
        for base, mat, inp, upref in ((0, r.tt, r.sf, r.up), (256, r.uu, r.sr, r.upj)):
            long_out = dot(mat[g], inp[:, here])
            g_pre = r.gate[base : base + 256, here]
            s = jax.nn.sigmoid(g_pre)
            ul = upref[:, here].astype(F32) * long_out
            r.gr[base : base + 256, here] = (g_pre * s * long_out).astype(BF)
            r.dg[base : base + 256, here] = (ul * s * (1.0 + g_pre * (1.0 - s))).astype(BF)
        return carry

    lax.fori_loop(0, 8, long_conv, 0)

    first, c_b, w_b = [], STARTS[1], WIDTHS[1]

    def part_b(i, carry):
        blk = dot(r.xt[pl.ds(pl.multiple_of(i * 256, 256), 256), :], r.dg[:, c_b : c_b + w_b])
        r.pb[i // 4, pl.ds(lax.rem(i, 4) * 8, 8)] = blk.astype(BF).reshape(8, 2, 16, w_b)
        return carry

    def part_c(i, carry):
        c, w = STARTS[2], WIDTHS[2]
        blk = dot(r.xt[pl.ds(pl.multiple_of(i * 256, 256), 256), :], r.dg[:, c : c + w])
        r.pc[pl.ds(i * 2, 2)] = blk.astype(BF).reshape(2, 4, 32, w)
        return carry

    def part_a(i, carry):
        c, w = STARTS[0], WIDTHS[0]
        blk = dot(r.xt[pl.ds(pl.multiple_of(i * 256, 256), 256), :], r.dg[:, c : c + w])
        r.pa[i // 4, lax.rem(i, 4)] = blk.astype(BF)
        return carry

    def send_x(src_of, dst):
        return [remote(src_of(lax.rem(x + o, 4)), dst.at[o - 1], x_peer(o)) for o in (1, 3, 2)]

    def send_y(src_of, dst):
        out = []
        for o in (1, 3, 2):
            t = lax.rem(y + o, 4)
            out.append(remote(src_of(lax.rem(t, 2), t // 2), dst.at[o - 1], y_peer(o)))
        return out

    def send_z(src_of, dst):
        return [remote(src_of(lax.rem(z + o, 4)), dst.at[o - 1], z_peer(o)) for o in (1, 3, 2)]

    lax.fori_loop(0, 8, part_b, 0)
    b1 = send_y(lambda lo, hi: r.pb.at[lo, :, hi], r.rb1)
    lax.fori_loop(0, 8, part_c, 0)
    c1 = send_z(lambda j: r.pc.at[:, j], r.rc1)
    lax.fori_loop(0, 8, part_a, 0)
    a1 = send_x(lambda j: r.pa.at[:, j], r.ra1)

    def mix(i, carry):
        here = pl.ds(pl.multiple_of(i * 256, 256), 256)
        there = pl.ds(pl.multiple_of(768 - i * 256, 256), 256)
        rev = dot(r.gr[256:512, there], r.jm[...])
        r.mx[:, here] = (r.gr[0:256, here].astype(F32) + rev).astype(BF)
        return carry

    lax.fori_loop(0, 4, mix, 0)
    tail_local, tail_remote = [], []
    for i in range(2):
        span = pl.ds(512 * i, 512)
        dst = mixed.at[0, :, pl.ds(offs[i], 512)]
        tail_local.append(local(r.mx.at[pl.ds(own, 128), span], dst))
        tail_remote.append(remote(r.mx.at[pl.ds(theirs, 128), span], dst, partner))

    rim_df.wait_recv()
    rim_dr.wait_recv()

    @pl.when(chip == 7)
    def _():
        r.df[256:512, :] = jnp.zeros((256, 1024), BF)

    @pl.when(chip == 0)
    def _():
        r.dr[0:256, :] = jnp.zeros((256, 1024), BF)

    sm_own = r.sm.at[0, x]
    sm_own[...] = jnp.zeros((8, SMALL), F32)

    def back_conv(g, carry):
        here = pl.ds(pl.multiple_of(g * 128, 128), 128)
        ds_f = dot(r.uu[g], r.df[:, here]).astype(BF)
        r.dsf[0:256, here] = ds_f
        ds_r = dot(r.tt[g], r.dr[:, here]).astype(BF)
        r.dsr[16:272, here] = ds_r
        lag_f = dot_nt(r.df[0:256, here], r.sf[:, here])
        r.ls[0, g] = skew_sum(lag_f, True)
        lag_r = dot_nt(r.dr[256:512, here], r.sr[:, here])
        r.ls[1, g] = skew_sum(lag_r, True)
        fwd = r.xf[:, here].astype(F32)
        rev = r.xr[:, here].astype(F32)
        ds_f32, ds_r32 = ds_f.astype(F32), ds_r.astype(F32)
        for k in range(4):
            xk = fwd[16:272] if k == 0 else pltpu.roll(fwd, k, 0)[16:272]
            rk = rev[0:256] if k == 0 else pltpu.roll(rev, 272 - k, 0)[0:256]
            sm_own[k : k + 1, here] = jnp.sum(ds_f32 * xk + ds_r32 * rk, axis=0, keepdims=True)
        return carry

    lax.fori_loop(0, 8, back_conv, 0)
    rim_dsf = remote(r.dsf.at[pl.ds(0, 16)], r.dsf.at[pl.ds(256, 16)], at_chip(prv, core))
    rim_dsr = remote(r.dsr.at[pl.ds(256, 16)], r.dsr.at[pl.ds(0, 16)], at_chip(nxt, core))

    sums = []
    for strand in range(2):
        total = r.ls[strand, :, 0, :]
        for t in range(1, 8):
            total = total + pltpu.roll(r.ls[strand, :, t, :], 512 - t, 1)
        sums.append(total)
    lag_m = lax.broadcasted_iota(jnp.int32, (512, 256), 0)
    lag_k = lax.broadcasted_iota(jnp.int32, (512, 256), 1)
    turned = jnp.dot(
        sums[0],
        jnp.where(lag_m + lag_k == 256, 1.0, 0.0),
        precision=lax.Precision.HIGHEST,
        preferred_element_type=F32,
    )
    sm_own[:, 1024:SMALL] = turned + sums[1][:, 0:256]
    small_x = [remote(r.sm.at[0, x], r.sm.at[0, x], x_peer(o)) for o in (1, 3, 2)]

    def d_input(i, carry):
        here = pl.ds(pl.multiple_of(i * 256, 256), 256)
        there = pl.ds(pl.multiple_of(1792 - i * 256, 256), 256)
        rev = dot_nt(r.dg[256:512, :], r.w[there, :]).astype(BF)
        r.dh[:, here] = dot_nt(r.dg[0:256, :], r.w[here, :]) + dot(rev, r.jm[...])
        return carry

    lax.fori_loop(0, 8, d_input, 0)

    rim_dsf.wait_recv()
    rim_dsr.wait_recv()

    @pl.when(chip == 7)
    def _():
        r.dsf[256:272, :] = jnp.zeros((16, 1024), BF)

    @pl.when(chip == 0)
    def _():
        r.dsr[0:16, :] = jnp.zeros((16, 1024), BF)

    def short_back(g, carry):
        here = pl.ds(pl.multiple_of(g * 128, 128), 128)
        there = pl.ds(col(g, 128), 128)
        fwd = r.dsf[:, here].astype(F32)
        rev = r.dsr[:, here].astype(F32)
        acc_f = r.st[0:1, there] * fwd[0:256]
        acc_r = r.st[0:1, there] * rev[16:272]
        for k in range(1, 4):
            tap = r.st[k : k + 1, there]
            acc_f += tap * pltpu.roll(fwd, 272 - k, 0)[0:256]
            acc_r += tap * pltpu.roll(rev, k, 0)[16:272]
        r.dh[:, there] = r.dh[:, there] + acc_f
        r.dxr[:, here] = acc_r.astype(BF)
        return carry

    lax.fori_loop(0, 8, short_back, 0)
    for i in range(4):
        there = pl.ds(col(i, 256), 256)
        r.dh[:, there] = r.dh[:, there] + dot(r.dxr[:, 768 - 256 * i : 1024 - 256 * i], r.jm[...])
    r.dhs[...] = r.dh[pl.ds(theirs, 128), :].astype(BF)
    pair_d = remote(r.dhs, r.dhr, partner)

    def summed(ref_own, ref_got, copies):
        for copy in copies:
            copy.wait_recv()
        total = ref_own[...].astype(F32)
        for o in range(3):
            total = total + ref_got[o].astype(F32)
        return total

    def add_stage(count_, own_at, got, copies, put):
        for copy in copies:
            copy.wait_recv()

        def step(i, carry):
            total = own_at(i).astype(F32)
            for o in range(3):
                total = total + got[o, i].astype(F32)
            put(i, total.astype(BF))
            return carry

        lax.fori_loop(0, count_, step, 0)

    def put_b1(i, v):
        r.sb1[i // 4, lax.rem(i, 4)] = v

    def put_c1(i, v):
        r.sc1[i // 8, lax.rem(i // 2, 4), pl.ds(pl.multiple_of(lax.rem(i, 2) * 32, 32), 32)] = v

    def put_a1(i, v):
        r.sa1[i] = v.reshape(8, 2, 16, WIDTHS[0])

    add_stage(32, lambda i: r.pb[y_lo, i, y_hi], r.rb1, b1, put_b1)
    b2 = send_z(lambda j: r.sb1.at[:, j], r.rb2)
    add_stage(16, lambda i: r.pc[i, z], r.rc1, c1, put_c1)
    c2 = send_x(lambda j: r.sc1.at[:, j], r.rc2)
    add_stage(2, lambda i: r.pa[i, x], r.ra1, a1, put_a1)
    a2 = send_y(lambda lo, hi: r.sa1.at[lo, :, hi], r.ra2)

    def small_sum(stage, copies):
        for copy in copies:
            copy.wait_recv()
        return (r.sm[stage, 0] + r.sm[stage, 1]) + (r.sm[stage, 2] + r.sm[stage, 3])

    r.sm[1, y] = small_sum(0, small_x)
    small_y = [remote(r.sm.at[1, y], r.sm.at[1, y], y_peer(o)) for o in (1, 3, 2)]

    pair_d.wait_recv()
    r.dho[...] = (r.dh[pl.ds(own, 128), :] + r.dhr[...].astype(F32)).astype(BF)
    tail_local.append(local(r.dho, dhid.at[0]))

    r.sb2[...] = summed(r.sb1.at[:, z], r.rb2, b2).astype(BF).reshape(4, 32, WIDTHS[1])
    b3 = send_x(lambda j: r.sb2.at[j], r.rb3)
    r.sc2[...] = summed(r.sc1.at[:, x], r.rc2, c2).astype(BF).reshape(2, 2, 2, 16, WIDTHS[2])
    c3 = send_y(lambda lo, hi: r.sc2.at[lo, :, hi], r.rc3)
    r.sa2[...] = summed(r.sa1.at[y_lo, :, y_hi], r.ra2, a2).astype(BF).reshape(2, 4, 16, WIDTHS[0])
    a3 = send_z(lambda j: r.sa2.at[:, j], r.ra3)

    r.sm[2, z] = small_sum(1, small_y)
    small_z = [remote(r.sm.at[2, z], r.sm.at[2, z], z_peer(o)) for o in (1, 3, 2)]

    def put_fin(part, value):
        r.fin[:, :, STARTS[part] : STARTS[part] + WIDTHS[part]] = value.reshape(2, 16, WIDTHS[part])

    put_fin(1, summed(r.sb2.at[x], r.rb3, b3))
    put_fin(2, summed(r.sc2.at[y_lo, :, y_hi], r.rc3, c3))
    put_fin(0, summed(r.sa2.at[:, z], r.ra3, a3))
    for i in range(2):
        span = pl.ds(512 * i, 512)
        dst = ggate.at[:, pl.ds(offs[i], 512)]
        tail_local.append(local(r.fin.at[core, :, span], dst))
        tail_remote.append(remote(r.fin.at[other, :, span], dst, partner))

    r.smo[...] = small_sum(2, small_z)
    tail_local.append(local(r.smo, small.at[core]))
    tail_remote.append(remote(r.smo, small.at[core], partner))

    for copy in tail_local:
        copy.wait()
    for copy in tail_remote:
        copy.wait_recv()
    for copy in started:
        copy.wait_send()


def body(hidden, short_taps, long_taps, gate_weight, upstream):
    outside = pl.BlockSpec(memory_space=pl.ANY)
    inside = pl.BlockSpec(memory_space=pltpu.VMEM)
    mixed, ggate, small, dhid = pl.pallas_call(
        kernel,
        out_shape=(
            jax.ShapeDtypeStruct((1, 128, 2048), BF),
            jax.ShapeDtypeStruct((16, 2048), F32),
            jax.ShapeDtypeStruct((2, 8, SMALL), F32),
            jax.ShapeDtypeStruct((1, 128, 2048), BF),
        ),
        in_specs=[outside, inside, inside, outside, outside],
        out_specs=(outside,) * 4,
        scratch_shapes=[pltpu.VMEM(shape, dtype) for shape, dtype in SCRATCH.values()]
        + [
            pltpu.SemaphoreType.DMA((LOCAL_SEMS,)),
            pltpu.SemaphoreType.DMA((REMOTE_SEMS,)),
            pltpu.SemaphoreType.DMA((REMOTE_SEMS,)),
        ],
        compiler_params=pltpu.CompilerParams(
            collective_id=0, has_side_effects=True, vmem_limit_bytes=60 * 1024 * 1024
        ),
        cost_estimate=pl.CostEstimate(
            flops=8 * 10**9, bytes_accessed=12 * 2**20, transcendentals=2**20
        ),
    )(hidden, short_taps, long_taps, gate_weight, upstream)
    edge, middle = small[1], small[0]
    grad_short = jnp.concatenate(
        [edge[0:4, 0:512], middle[0:4, 0:1024], edge[0:4, 512:1024]], axis=1
    )
    edge_lag, middle_lag = edge[:, 1024:], middle[:, 1024:]
    grad_long = jnp.transpose(jnp.concatenate([edge_lag[0:4], middle_lag, edge_lag[4:8]], axis=0))
    return (mixed, ggate, grad_short, grad_long, dhid)


def solution(mesh):
    placed = (P("dp", "seq", None), P(), P(), P(), P("dp", "seq", None))
    return jax.shard_map(
        body,
        mesh=mesh,
        in_specs=placed,
        out_specs=(P("dp", "seq", None), P(("seq", "dp"), None), P(), P(), P("dp", "seq", None)),
        check_vma=False,
    )
```

```python
import types

import jax
import jax.numpy as jnp
from jax import lax
from jax.experimental import pallas as pl
from jax.experimental.pallas import tpu as pltpu
from jax.sharding import PartitionSpec as P

BF = jnp.bfloat16
F32 = jnp.float32
MESH = pl.DeviceIdType.MESH
NT = (((1,), (1,)), ((), ()))

PARTS = (("z", 0, 384), ("y", 384, 128), ("z", 768, 256), ("y", 512, 128), ("x", 640, 128))
ROUTES = dict(
    x=("xyz", (2, 4, 256), (2, 8, 2, 16), (2, 4, 16), (2, 256), (8, 16), (2, 16)),
    y=("yzx", (2, 32, 2, 16), (8, 4, 16), (4, 32), (32, 16), (8, 16), (32,)),
    z=("zxy", (16, 4, 32), (2, 4, 64), (2, 2, 2, 16), (16, 32), (2, 64), (2, 16)),
)
RING = 4
SMALL = 1280

SCRATCH = dict(
    hh=((512, 2048), BF),
    w=((2048, 1024), BF),
    up=((256, 1024), BF),
    upj=((256, 1024), BF),
    halo=((2, 16, 2048), BF),
    st=((4, 2048), F32),
    xf=((528, 1024), BF),
    xr=((528, 1024), BF),
    xn=((256, 1024), BF),
    sf=((512, 1024), BF),
    sr=((512, 1024), BF),
    df=((512, 1024), BF),
    dr=((512, 1024), BF),
    gate=((512, 1024), F32),
    gr=((512, 1024), BF),
    mx=((256, 1024), BF),
    dg=((512, 1024), BF),
    tt=((8, 256, 512), BF),
    uu=((8, 256, 512), BF),
    tv=((16, 512), F32),
    uv=((16, 512), F32),
    jm=((256, 256), BF),
    im=((256, 256), BF),
    xt=((2048, 512), BF),
    fin=((2, 16, 1024), F32),
    dsf=((272, 1024), BF),
    dsr=((272, 1024), BF),
    ls=((2, 8, 8, 512), F32),
    sm=((3, 4, 8, SMALL), F32),
    smo=((8, SMALL), F32),
    dh=((256, 2048), F32),
    dxr=((256, 1024), BF),
    dhs=((128, 2048), BF),
    dhr=((128, 2048), BF),
    dho=((128, 2048), BF),
)
for n, (axis, _, columns) in enumerate(PARTS):
    _, *layouts = ROUTES[axis]
    for m, layout in enumerate(layouts):
        copies_ = () if m < 3 else (2,) if m == 3 else (3,)
        SCRATCH[f"{'pstabc'[m]}{n}"] = (copies_ + layout + (columns,), BF)
    SCRATCH[f"r{n}"] = ((2, layouts[3][0] // 2) + layouts[3][1:] + (columns,), BF)
LOCAL_SEMS = 16
REMOTE_SEMS = 110


def dot(a, b):
    return jnp.dot(a, b, preferred_element_type=F32)


def dot_nt(a, b):
    return lax.dot_general(a, b, NT, preferred_element_type=F32)


def skew_sum(m, to_left):
    rows, lanes = m.shape
    while rows > 8:
        rows //= 2
        shift = lanes - rows if to_left else rows
        m = m[:rows] + pltpu.roll(m[rows:], shift, 1)
    return m


def kernel(hidden, staps, ltaps, weight, upstream, mixed, ggate, small, dhid, *scratch):
    r = types.SimpleNamespace(**dict(zip(SCRATCH, scratch)))
    loc, send, recv = scratch[len(SCRATCH) :]

    seq, dp = lax.axis_index("seq"), lax.axis_index("dp")
    core = lax.rem(seq, 2)
    chip = seq // 2
    x = lax.rem(chip, 4)
    y_lo = chip // 4
    y_hi = lax.rem(dp, 2)
    y = y_hi * 2 + y_lo
    z = dp // 2
    other = 1 - core

    def at_chip(c, k):
        return {"seq": c * 2 + k, "dp": dp}

    def x_peer(o):
        return {"seq": (y_lo * 4 + lax.rem(x + o, 4)) * 2 + core, "dp": dp}

    def y_peer(o):
        t = lax.rem(y + o, 4)
        return {
            "seq": (lax.rem(t, 2) * 4 + x) * 2 + core,
            "dp": z * 2 + t // 2,
        }

    def z_peer(o):
        return {"seq": seq, "dp": lax.rem(z + o, 4) * 2 + y_hi}

    partner = at_chip(chip, other)
    nxt, prv = lax.rem(chip + 1, 8), lax.rem(chip + 7, 8)
    far_chip = lax.rem(chip + 6 + 4 * core, 8)
    peers = [partner]
    peers += [at_chip(lax.rem(chip + o, 8), k) for o in (1, 7, 2, 6) for k in range(2)]
    peers += [f(o) for f in (x_peer, y_peer, z_peer) for o in (1, 2, 3)]

    offs = [pl.multiple_of(512 * other, 512), pl.multiple_of(1024 + 512 * core, 512)]
    offs_other = [pl.multiple_of(512 * core, 512), pl.multiple_of(1024 + 512 * other, 512)]
    own = pl.multiple_of(core * 128, 128)
    theirs = pl.multiple_of(other * 128, 128)

    def col(g, width):
        half = 512 // width
        c = jnp.where(g < half, 512 * other + g * width, 512 + 512 * core + g * width)
        return pl.multiple_of(c, width)

    started = []
    count = [0]

    def remote(src, dst, device, recv_index=None):
        i = count[0]
        count[0] += 1
        copy = pltpu.make_async_remote_copy(
            src_ref=src,
            dst_ref=dst,
            send_sem=send.at[i],
            recv_sem=recv.at[i if recv_index is None else recv_index],
            device_id=device,
            device_id_type=MESH,
        )
        copy.start()
        started.append(copy)
        return copy

    lcount = [0]

    def local(src, dst):
        copy = pltpu.make_async_copy(src, dst, loc.at[lcount[0]])
        lcount[0] += 1
        copy.start()
        return copy

    in_h = local(hidden.at[0], r.hh.at[pl.ds(own, 128)])
    in_u = [
        local(
            upstream.at[0, :, pl.ds(offs[i], 512)],
            r.up.at[pl.ds(own, 128), pl.ds(512 * i, 512)],
        )
        for i in range(2)
    ]
    in_w = [
        local(weight.at[:, pl.ds(offs[i], 512)], r.w.at[:, pl.ds(512 * i, 512)])
        for i in range(2)
    ]

    barrier = pltpu.get_barrier_semaphore()
    for peer in peers:
        pl.semaphore_signal(barrier, inc=1, device_id=peer, device_id_type=MESH)

    pl.semaphore_wait(barrier, len(peers))
    base = REMOTE_SEMS
    pair_h = remote(hidden.at[0], r.hh.at[pl.ds(own, 128)], partner)

    def send_rims(wave):
        for k in range(2):
            for i, span, there in ((wave, 16 + own, True), (1 - wave, own, False)):
                off = (512 * (1 - k), 1024 + 512 * k)[i]
                src = hidden.at[0, :, pl.ds(off, 512)]
                at = (pl.ds(pl.multiple_of(span, 16), 128), pl.ds(512 * i, 512))
                index = base + (0 if there else 4) + core * 2 + i
                if there:
                    remote(src, r.xf.at[at], at_chip(nxt, k), index)
                else:
                    remote(src, r.xn.at[at], at_chip(prv, k), index)

    send_rims(0)
    halo_src = hidden.at[0, pl.ds(pl.multiple_of(core * 112, 16), 16)]
    for k in range(2):
        remote(halo_src, r.halo.at[other], at_chip(far_chip, k), base + 8 + other)
    pair_u = [
        remote(
            upstream.at[0, :, pl.ds(offs_other[i], 512)],
            r.up.at[pl.ds(own, 128), pl.ds(512 * i, 512)],
            partner,
        )
        for i in range(2)
    ]

    def arrived(src, dst, i):
        pltpu.make_async_remote_copy(
            src_ref=src,
            dst_ref=dst,
            send_sem=send.at[0],
            recv_sem=recv.at[base + i],
            device_id=partner,
            device_id_type=MESH,
        ).wait_recv()

    rows_i = lax.broadcasted_iota(jnp.int32, (256, 256), 0)
    cols_i = lax.broadcasted_iota(jnp.int32, (256, 256), 1)
    r.jm[...] = jnp.where(rows_i + cols_i == 255, 1.0, 0.0).astype(BF)
    r.im[...] = jnp.where(rows_i == cols_i, 1.0, 0.0).astype(BF)
    r.st[...] = staps[...].astype(F32)

    tap_i = lax.broadcasted_iota(jnp.int32, (256, 512), 0)
    lag_i = lax.broadcasted_iota(jnp.int32, (256, 512), 1)
    taps = ltaps[...]
    r.tv[...] = dot(taps, jnp.where(tap_i + lag_i == 256, 1.0, 0.0).astype(BF))
    r.uv[...] = dot(taps, jnp.where(tap_i == lag_i, 1.0, 0.0).astype(BF))

    def toeplitz(g, carry):
        gg = col(g, 128) // 128
        for vec, out in ((r.tv, r.tt), (r.uv, r.uu)):
            first = pltpu.roll(
                jnp.broadcast_to(vec[pl.ds(gg, 1), :], (32, 512)), 0, 1, stride=1, stride_axis=0
            )
            for b in range(8):
                block = first if b == 0 else pltpu.roll(first, 32 * b, 1)
                out[g, 32 * b : 32 * b + 32, :] = block.astype(BF)
        return carry


    in_h.wait()
    pair_h.wait_recv()

    def flip_rows(i, carry):
        here = pl.multiple_of(i * 256, 256)
        there = pl.multiple_of(1792 - i * 256, 256)
        r.hh[256:512, pl.ds(here, 256)] = dot(r.hh[0:256, pl.ds(there, 256)], r.jm[...]).astype(BF)
        return carry

    lax.fori_loop(0, 8, flip_rows, 0)

    for i in range(2):
        span = slice(512 * i, 512 * i + 512)
        r.xf[272:528, span] = r.hh[0:256, pl.ds(offs[i], 512)]
        r.xr[0:256, span] = r.hh[256:512, pl.ds(offs[i], 512)]

    send_rims(1)

    def short_conv(src_f, dst_f, src_r, dst_r, count_, wave):
        def step(g, carry):
            here = pl.ds(pl.multiple_of(g * 128, 128), 128)
            there = pl.ds(col(g, 128), 128)
            fwd = r.xf[src_f : src_f + count_ + 16, here].astype(F32)
            rev = r.xr[src_r : src_r + count_ + 16, here].astype(F32)
            acc_f = r.st[0:1, there] * fwd[16:]
            acc_r = r.st[0:1, there] * rev[:count_]
            for k in range(1, 4):
                tap = r.st[k : k + 1, there]
                acc_f += tap * pltpu.roll(fwd, k, 0)[16:]
                acc_r += tap * pltpu.roll(rev, count_ + 16 - k, 0)[:count_]
            r.sf[dst_f : dst_f + count_, here] = acc_f.astype(BF)
            r.sr[dst_r : dst_r + count_, here] = acc_r.astype(BF)
            return carry

        lax.fori_loop(4 * wave, 4 * wave + 4, step, 0)

    for copy in in_w + in_u:
        copy.wait()
    for copy in pair_u:
        copy.wait_recv()

    def gate_block(i, carry):
        here = pl.ds(pl.multiple_of(i * 256, 256), 256)
        there = pl.ds(pl.multiple_of(768 - i * 256, 256), 256)
        r.gate[:, here] = dot(r.hh[...], r.w[:, here])
        r.upj[:, here] = dot(r.up[:, there], r.jm[...]).astype(BF)

        def rows(b, carry):
            at = pl.multiple_of(b * 32, 32)
            gf = r.gate[pl.ds(at, 32), here]
            gb = r.gate[pl.ds(at + 256, 32), here]
            uf = r.up[pl.ds(at, 32), here].astype(F32)
            ub = r.upj[pl.ds(at, 32), here].astype(F32)
            r.df[pl.ds(at, 32), here] = (uf * gf * jax.nn.sigmoid(gf)).astype(BF)
            r.dr[pl.ds(at + 256, 32), here] = (ub * gb * jax.nn.sigmoid(gb)).astype(BF)
            return carry

        return lax.fori_loop(0, 8, rows, carry)

    def transposed(i, carry):
        here = pl.ds(pl.multiple_of(i * 256, 256), 256)
        r.xt[here, 0:256] = dot_nt(r.im[...], r.hh[0:256, here]).astype(BF)
        r.xt[here, 256:512] = dot_nt(r.im[...], r.hh[256:512, here]).astype(BF)
        return carry

    def flip_next(i, carry):
        here = pl.ds(pl.multiple_of(i * 256, 256), 256)
        there = pl.ds(pl.multiple_of(768 - i * 256, 256), 256)
        r.xr[256:512, here] = dot(r.xn[:, there], r.jm[...]).astype(BF)
        far = r.halo[1, :, pl.ds(col(3 - i, 256), 256)]
        r.xr[512:528, here] = dot(far, r.jm[...]).astype(BF)
        return carry

    def long_conv(g, carry):
        here = pl.ds(pl.multiple_of(g * 128, 128), 128)
        for start, mat, inp, upref in ((0, r.tt, r.sf, r.up), (256, r.uu, r.sr, r.upj)):
            long_out = dot(mat[g], inp[:, here])
            g_pre = r.gate[start : start + 256, here]
            s = jax.nn.sigmoid(g_pre)
            ul = upref[:, here].astype(F32) * long_out
            r.gr[start : start + 256, here] = (g_pre * s * long_out).astype(BF)
            r.dg[start : start + 256, here] = (ul * s * (1.0 + g_pre * (1.0 - s))).astype(BF)
        return carry

    def put_term(n, i, c, blk):
        axis, start, w = PARTS[n]
        ref = getattr(r, f"p{n}")
        lo, at = i // 2, lax.rem(i, 2) * 2
        first, last = max(c, start), min(c + 256, start + w)
        blk = blk[:, first - c : last - c].astype(BF)
        span, width = pl.ds(first - start, last - first), last - first
        if axis == "x":
            ref[lo, pl.ds(at, 2), :, span] = blk.reshape(2, 256, width)
        elif axis == "y":
            ref[lo, pl.ds(at * 8, 16), :, :, span] = blk.reshape(16, 2, 16, width)
        else:
            ref[pl.ds(i * 4, 4), :, :, span] = blk.reshape(4, 4, 32, width)

    def terms(c, *parts):
        def step(i, carry):
            at = pl.ds(pl.multiple_of(i * 512, 512), 512)
            blk = dot(r.xt[at, :], r.dg[:, c : c + 256])
            for n in parts:
                put_term(n, i, c, blk)
            return carry

        lax.fori_loop(0, 4, step, 0)

    def share(axis, ref, lead, o):
        if axis == "y":
            t = lax.rem(y + o, 4)
            return ref.at[lax.rem(t, 2), :, t // 2]
        t = lax.rem((x if axis == "x" else z) + o, 4)
        return ref.at[t] if lead == 0 else ref.at[:, t]

    peer_of = dict(x=x_peer, y=y_peer, z=z_peer)

    def across(axis, ref, lead, dst):
        return [
            remote(share(axis, ref, lead, o), dst.at[o - 1], peer_of[axis](o)) for o in (1, 3, 2)
        ]

    flight = {}

    def halves(ref):
        half = ref.shape[0] // 2
        return ref.at[pl.ds(0, half)], ref.at[pl.ds(half, half)]

    def start_ring(n):
        axis = PARTS[n][0]
        term, relay, got = (getattr(r, f"{c}{n}") for c in "pra")
        ahead, behind, far = (halves(share(axis, term, 1, o)) for o in (1, 3, 2))
        got_a, got_b = halves(got.at[0]), halves(got.at[1])
        up, down = peer_of[axis](1), peer_of[axis](3)
        relays = [remote(far[0], relay.at[0], up), remote(far[1], relay.at[1], down)]
        direct = [remote(ahead[1], got_a[1], up), remote(behind[0], got_b[0], down)]
        flight[n, "relay"] = relays
        flight[n, 0] = direct

    def pass_on(n):
        axis = PARTS[n][0]
        term, relay, got = (getattr(r, f"{c}{n}") for c in "pra")
        ahead, behind = (halves(share(axis, term, 1, o)) for o in (1, 3))
        got_a, got_b = halves(got.at[0]), halves(got.at[1])
        up, down = peer_of[axis](1), peer_of[axis](3)
        for i, (held, dst, peer) in enumerate(((ahead[0], got_a[0], up), (behind[1], got_b[1], down))):
            flight[n, "relay"][i].wait_recv()
            held[...] = (held[...].astype(F32) + relay[i].astype(F32)).astype(BF)
            flight[n, 0].append(remote(held, dst, peer))

    def start_stage(n, stage):
        axis = ROUTES[PARTS[n][0]][0][stage]
        ref = getattr(r, f"{'pst'[stage]}{n}")
        lead = len(ref.shape) - 3 if stage == 2 else 1
        flight[n, stage] = across(axis, ref, lead, getattr(r, f"{'abc'[stage]}{n}"))

    def end_stage(n, stage):
        axis = ROUTES[PARTS[n][0]][0][stage]
        w = PARTS[n][2]
        for copy in flight[n, stage]:
            copy.wait_recv()
        ref = getattr(r, f"{'pst'[stage]}{n}")
        got = getattr(r, f"{'abc'[stage]}{n}")
        held = share(axis, ref, len(ref.shape) - 3 if stage == 2 else 1, 0)
        if stage == 0:
            out = getattr(r, f"s{n}")
            steps, rows = {"x": (2, 256), "y": (32, 16), "z": (16, 32)}[axis]
            batch = 256 // rows

            def step(b, carry):
                at = pl.ds(b * batch, batch)
                total = held[at].astype(F32)
                for o in range(2):
                    total = total + got[o, at].astype(F32)
                total = total.astype(BF)
                if axis == "x":
                    out[pl.ds(b, 1)] = total.reshape(1, 8, 2, 16, w)
                elif axis == "y":
                    out[pl.ds(b * 4, 4)] = total.reshape(4, 4, 16, w)
                else:
                    out[pl.ds(b, 1)] = total.reshape(1, 4, 64, w)
                return carry

            lax.fori_loop(0, 2, step, 0)
            return
        total = held[...].astype(F32)
        for o in range(3):
            total = total + got[o].astype(F32)
        if stage == 1:
            out = getattr(r, f"t{n}")
            out[...] = total.astype(BF).reshape(out.shape)
        else:
            c = PARTS[n][1]
            r.fin[:, :, c : c + w] = total.reshape(2, 16, w)

    rims_d = []
    for wave in range(2):
        half = pl.ds(512 * wave, 512)
        span = slice(512 * wave, 512 * wave + 512)
        lax.fori_loop(2 * wave, 2 * wave + 2, gate_block, 0)
        df_at, dr_at = r.df.at[pl.ds(0, 256), half], r.dr.at[pl.ds(256, 256), half]
        rims_d.append(remote(df_at, r.df.at[pl.ds(256, 256), half], at_chip(prv, core)))
        rims_d.append(remote(dr_at, r.dr.at[pl.ds(0, 256), half], at_chip(nxt, core)))
        short_conv(272, 272, 0, 0, 240, wave)
        if wave == 0:
            lax.fori_loop(0, 8, toeplitz, 0)
            lax.fori_loop(0, 8, transposed, 0)
            for k in range(2):
                arrived(halo_src, r.halo.at[k], 8 + k)
            for i in range(2):
                r.xf[0:16, 512 * i : 512 * i + 512] = r.halo[0, :, pl.ds(offs[i], 512)]
        back = pl.ds(512 * (1 - wave), 512)
        for k in range(2):
            src = hidden.at[0, :, pl.ds(0, 512)]
            arrived(src, r.xf.at[pl.ds(16 + 128 * k, 128), half], k * 2 + wave)
            arrived(src, r.xn.at[pl.ds(128 * k, 128), back], 4 + k * 2 + 1 - wave)
        lax.fori_loop(2 * wave, 2 * wave + 2, flip_next, 0)

        @pl.when(chip == 0)
        def _():
            r.xf[0:272, span] = jnp.zeros((272, 512), BF)

        @pl.when(chip == 1)
        def _():
            r.xf[0:16, span] = jnp.zeros((16, 512), BF)

        @pl.when(chip == 7)
        def _():
            r.xr[256:528, span] = jnp.zeros((272, 512), BF)

        @pl.when(chip == 6)
        def _():
            r.xr[512:528, span] = jnp.zeros((16, 512), BF)

        short_conv(0, 0, 240, 240, 272, wave)
        lax.fori_loop(4 * wave, 4 * wave + 4, long_conv, 0)
        for c in ((0, 256), (768, 512))[wave]:
            terms(c, *[n for n, (_, b, w) in enumerate(PARTS) if b < c + 256 and c < b + w])
            for n in {256: (0, 1), 768: (2,), 512: (3, 4)}.get(c, ()):
                start_ring(n)
    for n in (0, 1):
        pass_on(n)

    def mix(i, carry):
        here = pl.ds(pl.multiple_of(i * 256, 256), 256)
        there = pl.ds(pl.multiple_of(768 - i * 256, 256), 256)
        rev = dot(r.gr[256:512, there], r.jm[...])
        r.mx[:, here] = (r.gr[0:256, here].astype(F32) + rev).astype(BF)
        return carry

    lax.fori_loop(0, 4, mix, 0)
    tail_local, tail_remote = [], []
    for i in range(2):
        span = pl.ds(512 * i, 512)
        dst = mixed.at[0, :, pl.ds(offs[i], 512)]
        tail_local.append(local(r.mx.at[pl.ds(own, 128), span], dst))
        tail_remote.append(remote(r.mx.at[pl.ds(theirs, 128), span], dst, partner))

    for n in (2, 3, 4):
        pass_on(n)
    for n in (0, 1):
        end_stage(n, 0)
        start_stage(n, 1)

    for copy in rims_d:
        copy.wait_recv()

    @pl.when(chip == 7)
    def _():
        r.df[256:512, :] = jnp.zeros((256, 1024), BF)

    @pl.when(chip == 0)
    def _():
        r.dr[0:256, :] = jnp.zeros((256, 1024), BF)

    sm_own = r.sm.at[0, x]
    sm_own[...] = jnp.zeros((8, SMALL), F32)

    def back_conv(g, carry):
        here = pl.ds(pl.multiple_of(g * 128, 128), 128)
        ds_f = dot(r.uu[g], r.df[:, here]).astype(BF)
        r.dsf[0:256, here] = ds_f
        ds_r = dot(r.tt[g], r.dr[:, here]).astype(BF)
        r.dsr[16:272, here] = ds_r
        lag_f = dot_nt(r.df[0:256, here], r.sf[:, here])
        r.ls[0, g] = skew_sum(lag_f, True)
        lag_r = dot_nt(r.dr[256:512, here], r.sr[:, here])
        r.ls[1, g] = skew_sum(lag_r, True)
        fwd = r.xf[256:528, here].astype(F32)
        rev = r.xr[0:272, here].astype(F32)
        ds_f32, ds_r32 = ds_f.astype(F32), ds_r.astype(F32)
        for k in range(4):
            xk = fwd[16:272] if k == 0 else pltpu.roll(fwd, k, 0)[16:272]
            rk = rev[0:256] if k == 0 else pltpu.roll(rev, 272 - k, 0)[0:256]
            sm_own[k : k + 1, here] = jnp.sum(ds_f32 * xk + ds_r32 * rk, axis=0, keepdims=True)
        return carry

    lax.fori_loop(0, 8, back_conv, 0)
    rim_dsf = remote(r.dsf.at[pl.ds(0, 16)], r.dsf.at[pl.ds(256, 16)], at_chip(prv, core))
    rim_dsr = remote(r.dsr.at[pl.ds(256, 16)], r.dsr.at[pl.ds(0, 16)], at_chip(nxt, core))

    sums = []
    for strand in range(2):
        total = r.ls[strand, :, 0, :]
        for t in range(1, 8):
            total = total + pltpu.roll(r.ls[strand, :, t, :], 512 - t, 1)
        sums.append(total)
    lag_m = lax.broadcasted_iota(jnp.int32, (512, 256), 0)
    lag_k = lax.broadcasted_iota(jnp.int32, (512, 256), 1)
    turned = jnp.dot(
        sums[0],
        jnp.where(lag_m + lag_k == 256, 1.0, 0.0),
        precision=lax.Precision.HIGHEST,
        preferred_element_type=F32,
    )
    sm_own[:, 1024:SMALL] = turned + sums[1][:, 0:256]
    small_x = [remote(r.sm.at[0, x], r.sm.at[0, x], x_peer(o)) for o in (1, 3, 2)]

    for n in (2, 3, 4):
        end_stage(n, 0)
        start_stage(n, 1)
    for n in (0, 1):
        end_stage(n, 1)
        start_stage(n, 2)

    def small_sum(stage, copies):
        for copy in copies:
            copy.wait_recv()
        return (r.sm[stage, 0] + r.sm[stage, 1]) + (r.sm[stage, 2] + r.sm[stage, 3])

    r.sm[1, y] = small_sum(0, small_x)
    small_y = [remote(r.sm.at[1, y], r.sm.at[1, y], y_peer(o)) for o in (1, 3, 2)]

    def d_input(i, carry):
        here = pl.ds(pl.multiple_of(i * 256, 256), 256)
        there = pl.ds(pl.multiple_of(1792 - i * 256, 256), 256)
        rev = dot_nt(r.dg[256:512, :], r.w[there, :]).astype(BF)
        r.dh[:, here] = dot_nt(r.dg[0:256, :], r.w[here, :]) + dot(rev, r.jm[...])
        return carry

    lax.fori_loop(0, 4, d_input, 0)
    for n in (2, 3, 4):
        end_stage(n, 1)
        start_stage(n, 2)
    r.sm[2, z] = small_sum(1, small_y)
    small_z = [remote(r.sm.at[2, z], r.sm.at[2, z], z_peer(o)) for o in (1, 3, 2)]
    lax.fori_loop(4, 8, d_input, 0)

    rim_dsf.wait_recv()
    rim_dsr.wait_recv()

    @pl.when(chip == 7)
    def _():
        r.dsf[256:272, :] = jnp.zeros((16, 1024), BF)

    @pl.when(chip == 0)
    def _():
        r.dsr[0:16, :] = jnp.zeros((16, 1024), BF)

    def short_back(g, carry):
        here = pl.ds(pl.multiple_of(g * 128, 128), 128)
        there = pl.ds(col(g, 128), 128)
        fwd = r.dsf[:, here].astype(F32)
        rev = r.dsr[:, here].astype(F32)
        acc_f = r.st[0:1, there] * fwd[0:256]
        acc_r = r.st[0:1, there] * rev[16:272]
        for k in range(1, 4):
            tap = r.st[k : k + 1, there]
            acc_f += tap * pltpu.roll(fwd, 272 - k, 0)[0:256]
            acc_r += tap * pltpu.roll(rev, k, 0)[16:272]
        r.dh[:, there] = r.dh[:, there] + acc_f
        r.dxr[:, here] = acc_r.astype(BF)
        return carry

    lax.fori_loop(0, 8, short_back, 0)
    for i in range(4):
        there = pl.ds(col(i, 256), 256)
        r.dh[:, there] = r.dh[:, there] + dot(r.dxr[:, 768 - 256 * i : 1024 - 256 * i], r.jm[...])
    r.dhs[...] = r.dh[pl.ds(theirs, 128), :].astype(BF)
    pair_d = remote(r.dhs, r.dhr, partner)

    pair_d.wait_recv()
    r.dho[...] = (r.dh[pl.ds(own, 128), :] + r.dhr[...].astype(F32)).astype(BF)
    tail_local.append(local(r.dho, dhid.at[0]))
    for n in range(5):
        end_stage(n, 2)
    for i in range(2):
        span = pl.ds(512 * i, 512)
        dst = ggate.at[:, pl.ds(offs[i], 512)]
        tail_local.append(local(r.fin.at[core, :, span], dst))
        tail_remote.append(remote(r.fin.at[other, :, span], dst, partner))

    r.smo[...] = small_sum(2, small_z)
    tail_local.append(local(r.smo, small.at[core]))
    tail_remote.append(remote(r.smo, small.at[core], partner))

    for copy in tail_local:
        copy.wait()
    for copy in tail_remote:
        copy.wait_recv()
    for copy in started:
        copy.wait_send()


def finish(mixed, ggate, small, dhid, mixed_out, ggate_out, dhid_out, short_out, long_out, *rest):
    sems = rest[-1]
    held = rest[:3]
    reads = [
        pltpu.make_async_copy(src, dst, sems.at[i])
        for i, (src, dst) in enumerate(zip((mixed, dhid, ggate), held))
    ]
    writes = [
        pltpu.make_async_copy(src, dst, sems.at[3 + i])
        for i, (src, dst) in enumerate(zip(held, (mixed_out, dhid_out, ggate_out)))
    ]
    small_v = rest[3]
    read_small = pltpu.make_async_copy(small, small_v, sems.at[6])
    read_small.start()
    for copy in reads:
        copy.start()
    read_small.wait()
    small = small_v
    short_out[:, 0:512] = small[1, 0:4, 0:512]
    short_out[:, 512:1536] = small[0, 0:4, 0:1024]
    short_out[:, 1536:2048] = small[1, 0:4, 512:1024]
    long_out[0:4, :] = small[1, 0:4, 1024:SMALL]
    long_out[4:12, :] = small[0, :, 1024:SMALL]
    long_out[12:16, :] = small[1, 4:8, 1024:SMALL]
    for read, write in zip(reads, writes):
        read.wait()
        write.start()
    for write in writes:
        write.wait()


def body(hidden, short_taps, long_taps, gate_weight, upstream):
    outside = pl.BlockSpec(memory_space=pl.ANY)
    inside = pl.BlockSpec(memory_space=pltpu.VMEM)
    block = jax.ShapeDtypeStruct((1, 128, 2048), BF)
    gate_rows = jax.ShapeDtypeStruct((16, 2048), F32)
    mixed, ggate, small, dhid = pl.pallas_call(
        kernel,
        out_shape=(block, gate_rows, jax.ShapeDtypeStruct((2, 8, SMALL), F32), block),
        in_specs=[outside, inside, inside, outside, outside],
        out_specs=(outside,) * 4,
        scratch_shapes=[pltpu.VMEM(shape, dtype) for shape, dtype in SCRATCH.values()]
        + [
            pltpu.SemaphoreType.DMA((LOCAL_SEMS,)),
            pltpu.SemaphoreType.DMA((REMOTE_SEMS,)),
            pltpu.SemaphoreType.DMA((REMOTE_SEMS + 10,)),
        ],
        compiler_params=pltpu.CompilerParams(
            collective_id=0, has_side_effects=True, vmem_limit_bytes=60 * 1024 * 1024
        ),
        cost_estimate=pl.CostEstimate(
            flops=8 * 10**9, bytes_accessed=12 * 2**20, transcendentals=2**20
        ),
    )(hidden, short_taps, jnp.transpose(long_taps), gate_weight, upstream)
    mixed, ggate, dhid, grad_short, grad_long = pl.pallas_call(
        finish,
        out_shape=(
            block,
            gate_rows,
            block,
            jax.ShapeDtypeStruct((4, 2048), F32),
            jax.ShapeDtypeStruct((16, 256), F32),
        ),
        in_specs=[outside] * 4,
        out_specs=(outside, outside, outside, inside, inside),
        scratch_shapes=[
            pltpu.VMEM((1, 128, 2048), BF),
            pltpu.VMEM((1, 128, 2048), BF),
            pltpu.VMEM((16, 2048), F32),
            pltpu.VMEM((2, 8, SMALL), F32),
            pltpu.SemaphoreType.DMA((7,)),
        ],
        compiler_params=pltpu.CompilerParams(vmem_limit_bytes=60 * 1024 * 1024),
    )(mixed, ggate, small, dhid)
    return (mixed, ggate, grad_short, jnp.transpose(grad_long), dhid)


def solution(mesh):
    placed = (P("dp", "seq", None), P(), P(), P(), P("dp", "seq", None))
    return jax.shard_map(
        body,
        mesh=mesh,
        in_specs=placed,
        out_specs=(P("dp", "seq", None), P(("seq", "dp"), None), P(), P(), P("dp", "seq", None)),
        check_vma=False,
    )
```

```python
import types

import jax
import jax.numpy as jnp
from jax import lax
from jax.experimental import pallas as pl
from jax.experimental.pallas import tpu as pltpu
from jax.sharding import PartitionSpec as P

BF = jnp.bfloat16
F32 = jnp.float32
MESH = pl.DeviceIdType.MESH
NT = (((1,), (1,)), ((), ()))

PARTS = (("z", 0, 384), ("y", 384, 128), ("z", 768, 256), ("y", 512, 128), ("x", 640, 128))
ROUTES = dict(
    x=("xyz", (2, 4, 256), (2, 8, 2, 16), (2, 4, 16), (2, 256), (8, 16), (2, 16)),
    y=("yzx", (2, 32, 2, 16), (8, 4, 16), (4, 32), (32, 16), (8, 16), (32,)),
    z=("zxy", (16, 4, 32), (2, 4, 64), (2, 2, 2, 16), (16, 32), (2, 64), (2, 16)),
)
RING = 4
SMALL = 768

SCRATCH = dict(
    hh=((512, 2048), BF),
    w=((2048, 1024), BF),
    up=((256, 1024), BF),
    upj=((256, 1024), BF),
    halo=((2, 16, 2048), BF),
    st=((4, 2048), F32),
    xf=((528, 1024), BF),
    xr=((528, 1024), BF),
    xn=((256, 1024), BF),
    sf=((512, 1024), BF),
    sr=((512, 1024), BF),
    df=((512, 1024), BF),
    dr=((512, 1024), BF),
    gate=((512, 1024), F32),
    gr=((512, 1024), BF),
    mx=((256, 1024), BF),
    dg=((512, 1024), BF),
    tt=((8, 256, 512), BF),
    uu=((8, 256, 512), BF),
    tv=((16, 512), F32),
    uv=((16, 512), F32),
    jm=((256, 256), BF),
    im=((256, 256), BF),
    xt=((2048, 512), BF),
    fin=((2, 16, 1024), F32),
    dsf=((272, 1024), BF),
    dsr=((272, 1024), BF),
    ls=((2, 8, 8, 512), F32),
    sm=((3, 4, 8, SMALL), F32),
    smo=((8, SMALL), F32),
    dh=((256, 2048), F32),
    dxr=((256, 1024), BF),
    dhs=((128, 2048), BF),
    dhr=((128, 2048), BF),
    dho=((128, 2048), BF),
)
for n, (axis, _, columns) in enumerate(PARTS):
    _, *layouts = ROUTES[axis]
    for m, layout in enumerate(layouts):
        copies_ = () if m < 3 else (2,) if m == 3 else (3,)
        SCRATCH[f"{'pstabc'[m]}{n}"] = (copies_ + layout + (columns,), BF)
    SCRATCH[f"r{n}"] = ((2, layouts[3][0] // 2) + layouts[3][1:] + (columns,), BF)
LOCAL_SEMS = 16
REMOTE_SEMS = 110


def dot(a, b):
    return jnp.dot(a, b, preferred_element_type=F32)


def dot_nt(a, b):
    return lax.dot_general(a, b, NT, preferred_element_type=F32)


def skew_sum(m, to_left):
    rows, lanes = m.shape
    while rows > 8:
        rows //= 2
        shift = lanes - rows if to_left else rows
        m = m[:rows] + pltpu.roll(m[rows:], shift, 1)
    return m


def kernel(hidden, staps, ltaps, weight, upstream, mixed, ggate, small, dhid, *scratch):
    r = types.SimpleNamespace(**dict(zip(SCRATCH, scratch)))
    loc, send, recv = scratch[len(SCRATCH) :]

    seq, dp = lax.axis_index("seq"), lax.axis_index("dp")
    core = lax.rem(seq, 2)
    chip = seq // 2
    x = lax.rem(chip, 4)
    y_lo = chip // 4
    y_hi = lax.rem(dp, 2)
    y = y_hi * 2 + y_lo
    z = dp // 2
    other = 1 - core

    def at_chip(c, k):
        return {"seq": c * 2 + k, "dp": dp}

    def x_peer(o):
        return {"seq": (y_lo * 4 + lax.rem(x + o, 4)) * 2 + core, "dp": dp}

    def y_peer(o):
        t = lax.rem(y + o, 4)
        return {
            "seq": (lax.rem(t, 2) * 4 + x) * 2 + core,
            "dp": z * 2 + t // 2,
        }

    def z_peer(o):
        return {"seq": seq, "dp": lax.rem(z + o, 4) * 2 + y_hi}

    partner = at_chip(chip, other)
    nxt, prv = lax.rem(chip + 1, 8), lax.rem(chip + 7, 8)
    far_chip = lax.rem(chip + 6 + 4 * core, 8)
    peers = [partner]
    peers += [at_chip(lax.rem(chip + o, 8), k) for o in (1, 7, 2, 6) for k in range(2)]
    peers += [f(o) for f in (x_peer, y_peer, z_peer) for o in (1, 2, 3)]

    offs = [pl.multiple_of(512 * other, 512), pl.multiple_of(1024 + 512 * core, 512)]
    offs_other = [pl.multiple_of(512 * core, 512), pl.multiple_of(1024 + 512 * other, 512)]
    own = pl.multiple_of(core * 128, 128)
    theirs = pl.multiple_of(other * 128, 128)

    def col(g, width):
        half = 512 // width
        c = jnp.where(g < half, 512 * other + g * width, 512 + 512 * core + g * width)
        return pl.multiple_of(c, width)

    started = []
    count = [0]

    def remote(src, dst, device, recv_index=None):
        i = count[0]
        count[0] += 1
        copy = pltpu.make_async_remote_copy(
            src_ref=src,
            dst_ref=dst,
            send_sem=send.at[i],
            recv_sem=recv.at[i if recv_index is None else recv_index],
            device_id=device,
            device_id_type=MESH,
        )
        copy.start()
        started.append(copy)
        return copy

    lcount = [0]

    def local(src, dst):
        copy = pltpu.make_async_copy(src, dst, loc.at[lcount[0]])
        lcount[0] += 1
        copy.start()
        return copy

    in_h = local(hidden.at[0], r.hh.at[pl.ds(own, 128)])
    in_u = [
        local(
            upstream.at[0, :, pl.ds(offs[i], 512)],
            r.up.at[pl.ds(own, 128), pl.ds(512 * i, 512)],
        )
        for i in range(2)
    ]
    in_w = [
        local(weight.at[:, pl.ds(offs[i], 512)], r.w.at[:, pl.ds(512 * i, 512)])
        for i in range(2)
    ]

    barrier = pltpu.get_barrier_semaphore()
    for peer in peers:
        pl.semaphore_signal(barrier, inc=1, device_id=peer, device_id_type=MESH)

    pl.semaphore_wait(barrier, len(peers))
    base = REMOTE_SEMS
    pair_h = remote(hidden.at[0], r.hh.at[pl.ds(own, 128)], partner)

    def send_rims(wave):
        for k in range(2):
            for i, span, there in ((wave, 16 + own, True), (1 - wave, own, False)):
                off = (512 * (1 - k), 1024 + 512 * k)[i]
                src = hidden.at[0, :, pl.ds(off, 512)]
                at = (pl.ds(pl.multiple_of(span, 16), 128), pl.ds(512 * i, 512))
                index = base + (0 if there else 4) + core * 2 + i
                if there:
                    remote(src, r.xf.at[at], at_chip(nxt, k), index)
                else:
                    remote(src, r.xn.at[at], at_chip(prv, k), index)

    send_rims(0)
    halo_src = hidden.at[0, pl.ds(pl.multiple_of(core * 112, 16), 16)]
    for k in range(2):
        remote(halo_src, r.halo.at[other], at_chip(far_chip, k), base + 8 + other)
    pair_u = [
        remote(
            upstream.at[0, :, pl.ds(offs_other[i], 512)],
            r.up.at[pl.ds(own, 128), pl.ds(512 * i, 512)],
            partner,
        )
        for i in range(2)
    ]

    def arrived(src, dst, i):
        pltpu.make_async_remote_copy(
            src_ref=src,
            dst_ref=dst,
            send_sem=send.at[0],
            recv_sem=recv.at[base + i],
            device_id=partner,
            device_id_type=MESH,
        ).wait_recv()

    rows_i = lax.broadcasted_iota(jnp.int32, (256, 256), 0)
    cols_i = lax.broadcasted_iota(jnp.int32, (256, 256), 1)
    r.jm[...] = jnp.where(rows_i + cols_i == 255, 1.0, 0.0).astype(BF)
    r.im[...] = jnp.where(rows_i == cols_i, 1.0, 0.0).astype(BF)
    r.st[...] = staps[...].astype(F32)

    tap_i = lax.broadcasted_iota(jnp.int32, (256, 512), 0)
    lag_i = lax.broadcasted_iota(jnp.int32, (256, 512), 1)
    taps = ltaps[...]
    r.tv[...] = dot(taps, jnp.where(tap_i + lag_i == 256, 1.0, 0.0).astype(BF))
    r.uv[...] = dot(taps, jnp.where(tap_i == lag_i, 1.0, 0.0).astype(BF))

    def toeplitz(g, carry):
        gg = col(g, 128) // 128
        for vec, out in ((r.tv, r.tt), (r.uv, r.uu)):
            first = pltpu.roll(
                jnp.broadcast_to(vec[pl.ds(gg, 1), :], (32, 512)), 0, 1, stride=1, stride_axis=0
            )
            for b in range(8):
                block = first if b == 0 else pltpu.roll(first, 32 * b, 1)
                out[g, 32 * b : 32 * b + 32, :] = block.astype(BF)
        return carry


    in_h.wait()
    pair_h.wait_recv()

    def flip_rows(i, carry):
        here = pl.multiple_of(i * 256, 256)
        there = pl.multiple_of(1792 - i * 256, 256)
        r.hh[256:512, pl.ds(here, 256)] = dot(r.hh[0:256, pl.ds(there, 256)], r.jm[...]).astype(BF)
        return carry

    lax.fori_loop(0, 8, flip_rows, 0)

    for i in range(2):
        span = slice(512 * i, 512 * i + 512)
        r.xf[272:528, span] = r.hh[0:256, pl.ds(offs[i], 512)]
        r.xr[0:256, span] = r.hh[256:512, pl.ds(offs[i], 512)]

    send_rims(1)

    def short_conv(src_f, dst_f, src_r, dst_r, count_, wave):
        def step(g, carry):
            here = pl.ds(pl.multiple_of(g * 128, 128), 128)
            there = pl.ds(col(g, 128), 128)
            fwd = r.xf[src_f : src_f + count_ + 16, here].astype(F32)
            rev = r.xr[src_r : src_r + count_ + 16, here].astype(F32)
            acc_f = r.st[0:1, there] * fwd[16:]
            acc_r = r.st[0:1, there] * rev[:count_]
            for k in range(1, 4):
                tap = r.st[k : k + 1, there]
                acc_f += tap * pltpu.roll(fwd, k, 0)[16:]
                acc_r += tap * pltpu.roll(rev, count_ + 16 - k, 0)[:count_]
            r.sf[dst_f : dst_f + count_, here] = acc_f.astype(BF)
            r.sr[dst_r : dst_r + count_, here] = acc_r.astype(BF)
            return carry

        lax.fori_loop(4 * wave, 4 * wave + 4, step, 0)

    for copy in in_w + in_u:
        copy.wait()
    for copy in pair_u:
        copy.wait_recv()

    def gate_block(i, carry):
        here = pl.ds(pl.multiple_of(i * 256, 256), 256)
        there = pl.ds(pl.multiple_of(768 - i * 256, 256), 256)
        r.gate[:, here] = dot(r.hh[...], r.w[:, here])
        r.upj[:, here] = dot(r.up[:, there], r.jm[...]).astype(BF)

        def rows(b, carry):
            at = pl.multiple_of(b * 32, 32)
            gf = r.gate[pl.ds(at, 32), here]
            gb = r.gate[pl.ds(at + 256, 32), here]
            uf = r.up[pl.ds(at, 32), here].astype(F32)
            ub = r.upj[pl.ds(at, 32), here].astype(F32)
            r.df[pl.ds(at, 32), here] = (uf * gf * jax.nn.sigmoid(gf)).astype(BF)
            r.dr[pl.ds(at + 256, 32), here] = (ub * gb * jax.nn.sigmoid(gb)).astype(BF)
            return carry

        return lax.fori_loop(0, 8, rows, carry)

    def transposed(i, carry):
        here = pl.ds(pl.multiple_of(i * 256, 256), 256)
        r.xt[here, 0:256] = dot_nt(r.im[...], r.hh[0:256, here]).astype(BF)
        r.xt[here, 256:512] = dot_nt(r.im[...], r.hh[256:512, here]).astype(BF)
        return carry

    def flip_next(i, carry):
        here = pl.ds(pl.multiple_of(i * 256, 256), 256)
        there = pl.ds(pl.multiple_of(768 - i * 256, 256), 256)
        r.xr[256:512, here] = dot(r.xn[:, there], r.jm[...]).astype(BF)
        far = r.halo[1, :, pl.ds(col(3 - i, 256), 256)]
        r.xr[512:528, here] = dot(far, r.jm[...]).astype(BF)
        return carry

    def long_conv(g, carry):
        here = pl.ds(pl.multiple_of(g * 128, 128), 128)
        for start, mat, inp, upref in ((0, r.tt, r.sf, r.up), (256, r.uu, r.sr, r.upj)):
            long_out = dot(mat[g], inp[:, here])
            g_pre = r.gate[start : start + 256, here]
            s = jax.nn.sigmoid(g_pre)
            ul = upref[:, here].astype(F32) * long_out
            r.gr[start : start + 256, here] = (g_pre * s * long_out).astype(BF)
            r.dg[start : start + 256, here] = (ul * s * (1.0 + g_pre * (1.0 - s))).astype(BF)
        return carry

    def put_term(n, i, c, blk):
        axis, start, w = PARTS[n]
        ref = getattr(r, f"p{n}")
        lo, at = i // 2, lax.rem(i, 2) * 2
        first, last = max(c, start), min(c + 256, start + w)
        blk = blk[:, first - c : last - c].astype(BF)
        span, width = pl.ds(first - start, last - first), last - first
        if axis == "x":
            ref[lo, pl.ds(at, 2), :, span] = blk.reshape(2, 256, width)
        elif axis == "y":
            ref[lo, pl.ds(at * 8, 16), :, :, span] = blk.reshape(16, 2, 16, width)
        else:
            ref[pl.ds(i * 4, 4), :, :, span] = blk.reshape(4, 4, 32, width)

    def terms(c, *parts):
        def step(i, carry):
            at = pl.ds(pl.multiple_of(i * 512, 512), 512)
            blk = dot(r.xt[at, :], r.dg[:, c : c + 256])
            for n in parts:
                put_term(n, i, c, blk)
            return carry

        lax.fori_loop(0, 4, step, 0)

    def share(axis, ref, lead, o):
        if axis == "y":
            t = lax.rem(y + o, 4)
            return ref.at[lax.rem(t, 2), :, t // 2]
        t = lax.rem((x if axis == "x" else z) + o, 4)
        return ref.at[t] if lead == 0 else ref.at[:, t]

    peer_of = dict(x=x_peer, y=y_peer, z=z_peer)

    def across(axis, ref, lead, dst):
        return [
            remote(share(axis, ref, lead, o), dst.at[o - 1], peer_of[axis](o)) for o in (1, 3, 2)
        ]

    flight = {}

    def halves(ref):
        half = ref.shape[0] // 2
        return ref.at[pl.ds(0, half)], ref.at[pl.ds(half, half)]

    def start_ring(n):
        axis = PARTS[n][0]
        term, relay, got = (getattr(r, f"{c}{n}") for c in "pra")
        ahead, behind, far = (halves(share(axis, term, 1, o)) for o in (1, 3, 2))
        got_a, got_b = halves(got.at[0]), halves(got.at[1])
        up, down = peer_of[axis](1), peer_of[axis](3)
        relays = [remote(far[0], relay.at[0], up), remote(far[1], relay.at[1], down)]
        direct = [remote(ahead[1], got_a[1], up), remote(behind[0], got_b[0], down)]
        flight[n, "relay"] = relays
        flight[n, 0] = direct

    def pass_on(n):
        axis = PARTS[n][0]
        term, relay, got = (getattr(r, f"{c}{n}") for c in "pra")
        ahead, behind = (halves(share(axis, term, 1, o)) for o in (1, 3))
        got_a, got_b = halves(got.at[0]), halves(got.at[1])
        up, down = peer_of[axis](1), peer_of[axis](3)
        for i, (held, dst, peer) in enumerate(((ahead[0], got_a[0], up), (behind[1], got_b[1], down))):
            flight[n, "relay"][i].wait_recv()
            held[...] = (held[...].astype(F32) + relay[i].astype(F32)).astype(BF)
            flight[n, 0].append(remote(held, dst, peer))

    def start_stage(n, stage):
        axis = ROUTES[PARTS[n][0]][0][stage]
        ref = getattr(r, f"{'pst'[stage]}{n}")
        lead = len(ref.shape) - 3 if stage == 2 else 1
        flight[n, stage] = across(axis, ref, lead, getattr(r, f"{'abc'[stage]}{n}"))

    def end_stage(n, stage):
        axis = ROUTES[PARTS[n][0]][0][stage]
        w = PARTS[n][2]
        for copy in flight[n, stage]:
            copy.wait_recv()
        ref = getattr(r, f"{'pst'[stage]}{n}")
        got = getattr(r, f"{'abc'[stage]}{n}")
        held = share(axis, ref, len(ref.shape) - 3 if stage == 2 else 1, 0)
        if stage == 0:
            out = getattr(r, f"s{n}")
            steps, rows = {"x": (2, 256), "y": (32, 16), "z": (16, 32)}[axis]
            batch = 256 // rows

            def step(b, carry):
                at = pl.ds(b * batch, batch)
                total = held[at].astype(F32)
                for o in range(2):
                    total = total + got[o, at].astype(F32)
                total = total.astype(BF)
                if axis == "x":
                    out[pl.ds(b, 1)] = total.reshape(1, 8, 2, 16, w)
                elif axis == "y":
                    out[pl.ds(b * 4, 4)] = total.reshape(4, 4, 16, w)
                else:
                    out[pl.ds(b, 1)] = total.reshape(1, 4, 64, w)
                return carry

            lax.fori_loop(0, 2, step, 0)
            return
        total = held[...].astype(F32)
        for o in range(3):
            total = total + got[o].astype(F32)
        if stage == 1:
            out = getattr(r, f"t{n}")
            out[...] = total.astype(BF).reshape(out.shape)
        else:
            c = PARTS[n][1]
            r.fin[:, :, c : c + w] = total.reshape(2, 16, w)

    rims_d = []
    for wave in range(2):
        half = pl.ds(512 * wave, 512)
        span = slice(512 * wave, 512 * wave + 512)
        lax.fori_loop(2 * wave, 2 * wave + 2, gate_block, 0)
        df_at, dr_at = r.df.at[pl.ds(0, 256), half], r.dr.at[pl.ds(256, 256), half]
        rims_d.append(remote(df_at, r.df.at[pl.ds(256, 256), half], at_chip(prv, core)))
        rims_d.append(remote(dr_at, r.dr.at[pl.ds(0, 256), half], at_chip(nxt, core)))
        short_conv(272, 272, 0, 0, 240, wave)
        if wave == 0:
            lax.fori_loop(0, 8, toeplitz, 0)
            lax.fori_loop(0, 8, transposed, 0)
            for k in range(2):
                arrived(halo_src, r.halo.at[k], 8 + k)
            for i in range(2):
                r.xf[0:16, 512 * i : 512 * i + 512] = r.halo[0, :, pl.ds(offs[i], 512)]
        back = pl.ds(512 * (1 - wave), 512)
        for k in range(2):
            src = hidden.at[0, :, pl.ds(0, 512)]
            arrived(src, r.xf.at[pl.ds(16 + 128 * k, 128), half], k * 2 + wave)
            arrived(src, r.xn.at[pl.ds(128 * k, 128), back], 4 + k * 2 + 1 - wave)
        lax.fori_loop(2 * wave, 2 * wave + 2, flip_next, 0)

        @pl.when(chip == 0)
        def _():
            r.xf[0:272, span] = jnp.zeros((272, 512), BF)

        @pl.when(chip == 1)
        def _():
            r.xf[0:16, span] = jnp.zeros((16, 512), BF)

        @pl.when(chip == 7)
        def _():
            r.xr[256:528, span] = jnp.zeros((272, 512), BF)

        @pl.when(chip == 6)
        def _():
            r.xr[512:528, span] = jnp.zeros((16, 512), BF)

        short_conv(0, 0, 240, 240, 272, wave)
        lax.fori_loop(4 * wave, 4 * wave + 4, long_conv, 0)
        for c in ((0, 256), (768, 512))[wave]:
            terms(c, *[n for n, (_, b, w) in enumerate(PARTS) if b < c + 256 and c < b + w])
            for n in {256: (0, 1), 768: (2,), 512: (3, 4)}.get(c, ()):
                start_ring(n)
    for n in (0, 1):
        pass_on(n)

    def mix(i, carry):
        here = pl.ds(pl.multiple_of(i * 256, 256), 256)
        there = pl.ds(pl.multiple_of(768 - i * 256, 256), 256)
        rev = dot(r.gr[256:512, there], r.jm[...])
        r.mx[:, here] = (r.gr[0:256, here].astype(F32) + rev).astype(BF)
        return carry

    lax.fori_loop(0, 4, mix, 0)
    tail_local, tail_remote = [], []
    for i in range(2):
        span = pl.ds(512 * i, 512)
        dst = mixed.at[0, :, pl.ds(offs[i], 512)]
        tail_local.append(local(r.mx.at[pl.ds(own, 128), span], dst))
        tail_remote.append(remote(r.mx.at[pl.ds(theirs, 128), span], dst, partner))

    sm_own = r.sm.at[0, z]

    def back_conv(wave, g, carry):
        row, spot = 4 * wave, pl.ds(pl.multiple_of((g - 4 * wave) * 128, 128), 128)
        here = pl.ds(pl.multiple_of(g * 128, 128), 128)
        ds_f = dot(r.uu[g], r.df[:, here]).astype(BF)
        r.dsf[0:256, here] = ds_f
        ds_r = dot(r.tt[g], r.dr[:, here]).astype(BF)
        r.dsr[16:272, here] = ds_r
        lag_f = dot_nt(r.df[0:256, here], r.sf[:, here])
        r.ls[0, g] = skew_sum(lag_f, True)
        lag_r = dot_nt(r.dr[256:512, here], r.sr[:, here])
        r.ls[1, g] = skew_sum(lag_r, True)
        fwd = r.xf[256:528, here].astype(F32)
        rev = r.xr[0:272, here].astype(F32)
        ds_f32, ds_r32 = ds_f.astype(F32), ds_r.astype(F32)
        for k in range(4):
            xk = fwd[16:272] if k == 0 else pltpu.roll(fwd, k, 0)[16:272]
            rk = rev[0:256] if k == 0 else pltpu.roll(rev, 272 - k, 0)[0:256]
            total = jnp.sum(ds_f32 * xk + ds_r32 * rk, axis=0, keepdims=True)
            sm_own[row + k : row + k + 1, spot] = total
        return carry

    def d_input(i, carry):
        here = pl.ds(pl.multiple_of(i * 256, 256), 256)
        there = pl.ds(pl.multiple_of(1792 - i * 256, 256), 256)
        rev = dot_nt(r.dg[256:512, :], r.w[there, :]).astype(BF)
        r.dh[:, here] = dot_nt(r.dg[0:256, :], r.w[here, :]) + dot(rev, r.jm[...])
        return carry

    def rims_of(wave):
        span = slice(512 * wave, 512 * wave + 512)
        for copy in rims_d[2 * wave : 2 * wave + 2]:
            copy.wait_recv()

        @pl.when(chip == 7)
        def _():
            r.df[256:512, span] = jnp.zeros((256, 512), BF)

        @pl.when(chip == 0)
        def _():
            r.dr[0:256, span] = jnp.zeros((256, 512), BF)

    def stages(parts, stage):
        for n in parts:
            end_stage(n, stage)
            start_stage(n, stage + 1)

    small_axes = ((z, z_peer), (y, y_peer), (x, x_peer))

    def small_send(stage):
        at, peer = small_axes[stage]
        return [remote(r.sm.at[stage, at], r.sm.at[stage, at], peer(o)) for o in (1, 3, 2)]

    def small_sum(stage, copies):
        for copy in copies:
            copy.wait_recv()
        return (r.sm[stage, 0] + r.sm[stage, 1]) + (r.sm[stage, 2] + r.sm[stage, 3])

    rims_of(0)
    lax.fori_loop(0, 4, lambda g, carry: back_conv(0, g, carry), 0)
    lax.fori_loop(0, 4, d_input, 0)
    for n in (2, 3, 4):
        pass_on(n)
    stages((0, 1), 0)
    rims_of(1)
    lax.fori_loop(4, 8, lambda g, carry: back_conv(1, g, carry), 0)
    rim_dsf = remote(r.dsf.at[pl.ds(0, 16)], r.dsf.at[pl.ds(256, 16)], at_chip(prv, core))
    rim_dsr = remote(r.dsr.at[pl.ds(256, 16)], r.dsr.at[pl.ds(0, 16)], at_chip(nxt, core))

    sums = []
    for strand in range(2):
        total = r.ls[strand, :, 0, :]
        for t in range(1, 8):
            total = total + pltpu.roll(r.ls[strand, :, t, :], 512 - t, 1)
        sums.append(total)
    lag_m = lax.broadcasted_iota(jnp.int32, (512, 256), 0)
    lag_k = lax.broadcasted_iota(jnp.int32, (512, 256), 1)
    turned = jnp.dot(
        sums[0],
        jnp.where(lag_m + lag_k == 256, 1.0, 0.0),
        precision=lax.Precision.HIGHEST,
        preferred_element_type=F32,
    )
    sm_own[:, 512:SMALL] = turned + sums[1][:, 0:256]
    small_0 = small_send(0)
    stages((2, 3, 4), 0)
    lax.fori_loop(4, 6, d_input, 0)
    r.sm[1, y] = small_sum(0, small_0)
    small_1 = small_send(1)
    stages((0, 1), 1)
    lax.fori_loop(6, 8, d_input, 0)

    rim_dsf.wait_recv()
    rim_dsr.wait_recv()

    @pl.when(chip == 7)
    def _():
        r.dsf[256:272, :] = jnp.zeros((16, 1024), BF)

    @pl.when(chip == 0)
    def _():
        r.dsr[0:16, :] = jnp.zeros((16, 1024), BF)

    def short_back(g, carry):
        here = pl.ds(pl.multiple_of(g * 128, 128), 128)
        there = pl.ds(col(g, 128), 128)
        fwd = r.dsf[:, here].astype(F32)
        rev = r.dsr[:, here].astype(F32)
        acc_f = r.st[0:1, there] * fwd[0:256]
        acc_r = r.st[0:1, there] * rev[16:272]
        for k in range(1, 4):
            tap = r.st[k : k + 1, there]
            acc_f += tap * pltpu.roll(fwd, 272 - k, 0)[0:256]
            acc_r += tap * pltpu.roll(rev, k, 0)[16:272]
        r.dh[:, there] = r.dh[:, there] + acc_f
        r.dxr[:, here] = acc_r.astype(BF)
        return carry

    lax.fori_loop(0, 8, short_back, 0)
    for i in range(4):
        there = pl.ds(col(i, 256), 256)
        r.dh[:, there] = r.dh[:, there] + dot(r.dxr[:, 768 - 256 * i : 1024 - 256 * i], r.jm[...])
    r.dhs[...] = r.dh[pl.ds(theirs, 128), :].astype(BF)
    pair_d = remote(r.dhs, r.dhr, partner)

    r.sm[2, x] = small_sum(1, small_1)
    small_2 = small_send(2)
    stages((2, 3, 4), 1)

    pair_d.wait_recv()
    r.dho[...] = (r.dh[pl.ds(own, 128), :] + r.dhr[...].astype(F32)).astype(BF)
    tail_local.append(local(r.dho, dhid.at[0]))
    for n in range(5):
        end_stage(n, 2)
    for i in range(2):
        span = pl.ds(512 * i, 512)
        dst = ggate.at[:, pl.ds(offs[i], 512)]
        tail_local.append(local(r.fin.at[core, :, span], dst))
        tail_remote.append(remote(r.fin.at[other, :, span], dst, partner))

    r.smo[...] = small_sum(2, small_2)
    tail_local.append(local(r.smo, small.at[core]))
    tail_remote.append(remote(r.smo, small.at[core], partner))

    for copy in tail_local:
        copy.wait()
    for copy in tail_remote:
        copy.wait_recv()
    for copy in started:
        copy.wait_send()


def finish(mixed, ggate, small, dhid, mixed_out, ggate_out, dhid_out, short_out, long_out, *rest):
    sems = rest[-1]
    held = rest[:3]
    reads = [
        pltpu.make_async_copy(src, dst, sems.at[i])
        for i, (src, dst) in enumerate(zip((mixed, dhid, ggate), held))
    ]
    writes = [
        pltpu.make_async_copy(src, dst, sems.at[3 + i])
        for i, (src, dst) in enumerate(zip(held, (mixed_out, dhid_out, ggate_out)))
    ]
    small_v = rest[3]
    read_small = pltpu.make_async_copy(small, small_v, sems.at[6])
    read_small.start()
    for copy in reads:
        copy.start()
    read_small.wait()
    small = small_v
    for i, (half, row) in enumerate(((1, 0), (0, 0), (0, 4), (1, 4))):
        short_out[:, 512 * i : 512 * i + 512] = small[half, row : row + 4, 0:512]
    long_out[0:4, :] = small[1, 0:4, 512:SMALL]
    long_out[4:12, :] = small[0, :, 512:SMALL]
    long_out[12:16, :] = small[1, 4:8, 512:SMALL]
    for read, write in zip(reads, writes):
        read.wait()
        write.start()
    for write in writes:
        write.wait()


def body(hidden, short_taps, long_taps, gate_weight, upstream):
    outside = pl.BlockSpec(memory_space=pl.ANY)
    inside = pl.BlockSpec(memory_space=pltpu.VMEM)
    block = jax.ShapeDtypeStruct((1, 128, 2048), BF)
    gate_rows = jax.ShapeDtypeStruct((16, 2048), F32)
    mixed, ggate, small, dhid = pl.pallas_call(
        kernel,
        out_shape=(block, gate_rows, jax.ShapeDtypeStruct((2, 8, SMALL), F32), block),
        in_specs=[outside, inside, inside, outside, outside],
        out_specs=(outside,) * 4,
        scratch_shapes=[pltpu.VMEM(shape, dtype) for shape, dtype in SCRATCH.values()]
        + [
            pltpu.SemaphoreType.DMA((LOCAL_SEMS,)),
            pltpu.SemaphoreType.DMA((REMOTE_SEMS,)),
            pltpu.SemaphoreType.DMA((REMOTE_SEMS + 10,)),
        ],
        compiler_params=pltpu.CompilerParams(
            collective_id=0, has_side_effects=True, vmem_limit_bytes=60 * 1024 * 1024
        ),
        cost_estimate=pl.CostEstimate(
            flops=8 * 10**9, bytes_accessed=12 * 2**20, transcendentals=2**20
        ),
    )(hidden, short_taps, jnp.transpose(long_taps), gate_weight, upstream)
    mixed, ggate, dhid, grad_short, grad_long = pl.pallas_call(
        finish,
        out_shape=(
            block,
            gate_rows,
            block,
            jax.ShapeDtypeStruct((4, 2048), F32),
            jax.ShapeDtypeStruct((16, 256), F32),
        ),
        in_specs=[outside] * 4,
        out_specs=(outside, outside, outside, inside, inside),
        scratch_shapes=[
            pltpu.VMEM((1, 128, 2048), BF),
            pltpu.VMEM((1, 128, 2048), BF),
            pltpu.VMEM((16, 2048), F32),
            pltpu.VMEM((2, 8, SMALL), F32),
            pltpu.SemaphoreType.DMA((7,)),
        ],
        compiler_params=pltpu.CompilerParams(vmem_limit_bytes=60 * 1024 * 1024),
    )(mixed, ggate, small, dhid)
    return (mixed, ggate, grad_short, jnp.transpose(grad_long), dhid)


def solution(mesh):
    placed = (P("dp", "seq", None), P(), P(), P(), P("dp", "seq", None))
    return jax.shard_map(
        body,
        mesh=mesh,
        in_specs=placed,
        out_specs=(P("dp", "seq", None), P(("seq", "dp"), None), P(), P(), P("dp", "seq", None)),
        check_vma=False,
    )
```

```python
import types

import jax
import jax.numpy as jnp
from jax import lax
from jax.experimental import pallas as pl
from jax.experimental.pallas import tpu as pltpu
from jax.sharding import PartitionSpec as P

BF = jnp.bfloat16
F32 = jnp.float32
MESH = pl.DeviceIdType.MESH
NT = (((1,), (1,)), ((), ()))

PARTS = (("z", 0, 512, True), ("x", 768, 256, False), ("y", 512, 256, False))
EARLY = (0,)
LATE = tuple(range(1, len(PARTS)))
ROUTES = dict(
    x=("xyz", (2, 4, 256), (2, 8, 2, 16), (2, 4, 16), (2, 256), (8, 16), (2, 16)),
    y=("yzx", (2, 32, 2, 16), (8, 4, 16), (4, 32), (32, 16), (8, 16), (32,)),
    z=("zxy", (16, 4, 32), (2, 4, 64), (2, 2, 2, 16), (16, 32), (2, 64), (2, 16)),
)
RING = 4
SMALL = 768

SCRATCH = dict(
    hh=((512, 2048), BF),
    w=((2048, 1024), BF),
    up=((256, 1024), BF),
    upj=((256, 1024), BF),
    halo=((2, 16, 2048), BF),
    st=((4, 2048), F32),
    xf=((528, 1024), BF),
    xr=((528, 1024), BF),
    xn=((256, 1024), BF),
    sf=((512, 1024), BF),
    sr=((512, 1024), BF),
    df=((512, 1024), BF),
    dr=((512, 1024), BF),
    gate=((512, 1024), F32),
    gr=((512, 1024), BF),
    mx=((256, 1024), BF),
    dg=((512, 1024), BF),
    tt=((8, 256, 512), BF),
    uu=((8, 256, 512), BF),
    tv=((16, 512), F32),
    uv=((16, 512), F32),
    jm=((256, 256), BF),
    im=((256, 256), BF),
    xt=((2048, 512), BF),
    fin=((2, 16, 1024), F32),
    dsf=((272, 1024), BF),
    dsr=((272, 1024), BF),
    ls=((2, 8, 8, 512), F32),
    sm=((3, 4, 8, SMALL), F32),
    smo=((8, SMALL), F32),
    dh=((256, 2048), F32),
    dv=((256, 2048), BF),
    dxr=((256, 1024), BF),
    dhs=((128, 2048), BF),
    dhr=((128, 2048), BF),
    dho=((128, 2048), BF),
)
for n, (axis, _, columns, ring) in enumerate(PARTS):
    _, *layouts = ROUTES[axis]
    for m, layout in enumerate(layouts):
        copies_ = () if m < 3 else (2,) if m == 3 and ring else (3,)
        SCRATCH[f"{'pstabc'[m]}{n}"] = (copies_ + layout + (columns,), BF)
    if ring:
        SCRATCH[f"r{n}"] = ((2, layouts[3][0] // 2) + layouts[3][1:] + (columns,), BF)
LOCAL_SEMS = 16
REMOTE_SEMS = 110


def dot(a, b):
    return jnp.dot(a, b, preferred_element_type=F32)


def dot_nt(a, b):
    return lax.dot_general(a, b, NT, preferred_element_type=F32)


def skew_sum(m, to_left):
    rows, lanes = m.shape
    while rows > 8:
        rows //= 2
        shift = lanes - rows if to_left else rows
        m = m[:rows] + pltpu.roll(m[rows:], shift, 1)
    return m


def kernel(hidden, staps, ltaps, weight, upstream, mixed, ggate, small, dhid, *scratch):
    r = types.SimpleNamespace(**dict(zip(SCRATCH, scratch)))
    loc, send, recv = scratch[len(SCRATCH) :]

    seq, dp = lax.axis_index("seq"), lax.axis_index("dp")
    core = lax.rem(seq, 2)
    chip = seq // 2
    x = lax.rem(chip, 4)
    y_lo = chip // 4
    y_hi = lax.rem(dp, 2)
    y = y_hi * 2 + y_lo
    z = dp // 2
    other = 1 - core

    def at_chip(c, k):
        return {"seq": c * 2 + k, "dp": dp}

    def x_peer(o):
        return {"seq": (y_lo * 4 + lax.rem(x + o, 4)) * 2 + core, "dp": dp}

    def y_peer(o):
        t = lax.rem(y + o, 4)
        return {
            "seq": (lax.rem(t, 2) * 4 + x) * 2 + core,
            "dp": z * 2 + t // 2,
        }

    def z_peer(o):
        return {"seq": seq, "dp": lax.rem(z + o, 4) * 2 + y_hi}

    partner = at_chip(chip, other)
    nxt, prv = lax.rem(chip + 1, 8), lax.rem(chip + 7, 8)
    far_chip = lax.rem(chip + 6 + 4 * core, 8)
    peers = [partner]
    peers += [at_chip(lax.rem(chip + o, 8), k) for o in (1, 7, 2, 6) for k in range(2)]
    peers += [f(o) for f in (x_peer, y_peer, z_peer) for o in (1, 2, 3)]

    offs = [pl.multiple_of(512 * other, 512), pl.multiple_of(1024 + 512 * core, 512)]
    offs_other = [pl.multiple_of(512 * core, 512), pl.multiple_of(1024 + 512 * other, 512)]
    own = pl.multiple_of(core * 128, 128)
    theirs = pl.multiple_of(other * 128, 128)

    def col(g, width):
        half = 512 // width
        c = jnp.where(g < half, 512 * other + g * width, 512 + 512 * core + g * width)
        return pl.multiple_of(c, width)

    started = []
    count = [0]

    def remote(src, dst, device, recv_index=None):
        i = count[0]
        count[0] += 1
        copy = pltpu.make_async_remote_copy(
            src_ref=src,
            dst_ref=dst,
            send_sem=send.at[i],
            recv_sem=recv.at[i if recv_index is None else recv_index],
            device_id=device,
            device_id_type=MESH,
        )
        copy.start()
        started.append(copy)
        return copy

    lcount = [0]

    def local(src, dst):
        copy = pltpu.make_async_copy(src, dst, loc.at[lcount[0]])
        lcount[0] += 1
        copy.start()
        return copy

    in_h = local(hidden.at[0], r.hh.at[pl.ds(own, 128)])
    in_u = [
        local(
            upstream.at[0, :, pl.ds(offs[i], 512)],
            r.up.at[pl.ds(own, 128), pl.ds(512 * i, 512)],
        )
        for i in range(2)
    ]
    in_w = [
        local(weight.at[:, pl.ds(offs[i], 512)], r.w.at[:, pl.ds(512 * i, 512)])
        for i in range(2)
    ]

    barrier = pltpu.get_barrier_semaphore()
    for peer in peers:
        pl.semaphore_signal(barrier, inc=1, device_id=peer, device_id_type=MESH)

    pl.semaphore_wait(barrier, len(peers))
    base = REMOTE_SEMS
    pair_h = remote(hidden.at[0], r.hh.at[pl.ds(own, 128)], partner)

    def send_rims(wave):
        for k in range(2):
            for i, span, there in ((wave, 16 + own, True), (1 - wave, own, False)):
                off = (512 * (1 - k), 1024 + 512 * k)[i]
                src = hidden.at[0, :, pl.ds(off, 512)]
                at = (pl.ds(pl.multiple_of(span, 16), 128), pl.ds(512 * i, 512))
                index = base + (0 if there else 4) + core * 2 + i
                if there:
                    remote(src, r.xf.at[at], at_chip(nxt, k), index)
                else:
                    remote(src, r.xn.at[at], at_chip(prv, k), index)

    send_rims(0)
    halo_src = hidden.at[0, pl.ds(pl.multiple_of(core * 112, 16), 16)]
    for k in range(2):
        remote(halo_src, r.halo.at[other], at_chip(far_chip, k), base + 8 + other)
    pair_u = [
        remote(
            upstream.at[0, :, pl.ds(offs_other[i], 512)],
            r.up.at[pl.ds(own, 128), pl.ds(512 * i, 512)],
            partner,
        )
        for i in range(2)
    ]

    def arrived(src, dst, i):
        pltpu.make_async_remote_copy(
            src_ref=src,
            dst_ref=dst,
            send_sem=send.at[0],
            recv_sem=recv.at[base + i],
            device_id=partner,
            device_id_type=MESH,
        ).wait_recv()

    rows_i = lax.broadcasted_iota(jnp.int32, (256, 256), 0)
    cols_i = lax.broadcasted_iota(jnp.int32, (256, 256), 1)
    r.jm[...] = jnp.where(rows_i + cols_i == 255, 1.0, 0.0).astype(BF)
    r.im[...] = jnp.where(rows_i == cols_i, 1.0, 0.0).astype(BF)
    r.st[...] = staps[...].astype(F32)

    tap_i = lax.broadcasted_iota(jnp.int32, (256, 512), 0)
    lag_i = lax.broadcasted_iota(jnp.int32, (256, 512), 1)
    taps = ltaps[...]
    r.tv[...] = dot(taps, jnp.where(tap_i + lag_i == 256, 1.0, 0.0).astype(BF))
    r.uv[...] = dot(taps, jnp.where(tap_i == lag_i, 1.0, 0.0).astype(BF))

    def toeplitz(g, carry):
        gg = col(g, 128) // 128
        for vec, out in ((r.tv, r.tt), (r.uv, r.uu)):
            first = pltpu.roll(
                jnp.broadcast_to(vec[pl.ds(gg, 1), :], (32, 512)), 0, 1, stride=1, stride_axis=0
            )
            for b in range(8):
                block = first if b == 0 else pltpu.roll(first, 32 * b, 1)
                out[g, 32 * b : 32 * b + 32, :] = block.astype(BF)
        return carry


    lax.fori_loop(0, 8, toeplitz, 0)
    in_h.wait()
    pair_h.wait_recv()

    def flip_rows(i, carry):
        here = pl.multiple_of(i * 256, 256)
        there = pl.multiple_of(1792 - i * 256, 256)
        r.hh[256:512, pl.ds(here, 256)] = dot(r.hh[0:256, pl.ds(there, 256)], r.jm[...]).astype(BF)
        return carry

    lax.fori_loop(0, 8, flip_rows, 0)

    for i in range(2):
        span = slice(512 * i, 512 * i + 512)
        r.xf[272:528, span] = r.hh[0:256, pl.ds(offs[i], 512)]
        r.xr[0:256, span] = r.hh[256:512, pl.ds(offs[i], 512)]

    send_rims(1)

    def short_conv(src_f, dst_f, src_r, dst_r, count_, wave):
        def step(g, carry):
            here = pl.ds(pl.multiple_of(g * 128, 128), 128)
            there = pl.ds(col(g, 128), 128)
            fwd = r.xf[src_f : src_f + count_ + 16, here].astype(F32)
            rev = r.xr[src_r : src_r + count_ + 16, here].astype(F32)
            acc_f = r.st[0:1, there] * fwd[16:]
            acc_r = r.st[0:1, there] * rev[:count_]
            for k in range(1, 4):
                tap = r.st[k : k + 1, there]
                acc_f += tap * pltpu.roll(fwd, k, 0)[16:]
                acc_r += tap * pltpu.roll(rev, count_ + 16 - k, 0)[:count_]
            r.sf[dst_f : dst_f + count_, here] = acc_f.astype(BF)
            r.sr[dst_r : dst_r + count_, here] = acc_r.astype(BF)
            return carry

        lax.fori_loop(4 * wave, 4 * wave + 4, step, 0)

    for copy in in_w + in_u:
        copy.wait()
    for copy in pair_u:
        copy.wait_recv()

    def gate_block(i, carry):
        here = pl.ds(pl.multiple_of(i * 256, 256), 256)
        there = pl.ds(pl.multiple_of(768 - i * 256, 256), 256)
        r.gate[:, here] = dot(r.hh[...], r.w[:, here])
        r.upj[:, here] = dot(r.up[:, there], r.jm[...]).astype(BF)

        def rows(b, carry):
            at = pl.multiple_of(b * 32, 32)
            gf = r.gate[pl.ds(at, 32), here]
            gb = r.gate[pl.ds(at + 256, 32), here]
            uf = r.up[pl.ds(at, 32), here].astype(F32)
            ub = r.upj[pl.ds(at, 32), here].astype(F32)
            r.df[pl.ds(at, 32), here] = (uf * gf * jax.nn.sigmoid(gf)).astype(BF)
            r.dr[pl.ds(at + 256, 32), here] = (ub * gb * jax.nn.sigmoid(gb)).astype(BF)
            return carry

        return lax.fori_loop(0, 8, rows, carry, unroll=4)

    def transposed(i, carry):
        here = pl.ds(pl.multiple_of(i * 256, 256), 256)
        r.xt[here, 0:256] = dot_nt(r.im[...], r.hh[0:256, here]).astype(BF)
        return carry

    def transposed_flip(i, carry):
        here = pl.ds(pl.multiple_of(i * 256, 256), 256)
        there = pl.ds(pl.multiple_of(1792 - i * 256, 256), 256)
        r.xt[here, 256:512] = dot(r.jm[...], r.xt[there, 0:256]).astype(BF)
        return carry

    def flip_next(i, carry):
        here = pl.ds(pl.multiple_of(i * 256, 256), 256)
        there = pl.ds(pl.multiple_of(768 - i * 256, 256), 256)
        r.xr[256:512, here] = dot(r.xn[:, there], r.jm[...]).astype(BF)
        far = r.halo[1, :, pl.ds(col(3 - i, 256), 256)]
        r.xr[512:528, here] = dot(far, r.jm[...]).astype(BF)
        return carry

    def long_conv(g, carry):
        here = pl.ds(pl.multiple_of(g * 128, 128), 128)
        for start, mat, inp, upref in ((0, r.tt, r.sf, r.up), (256, r.uu, r.sr, r.upj)):
            long_out = dot(mat[g], inp[:, here])
            g_pre = r.gate[start : start + 256, here]
            s = jax.nn.sigmoid(g_pre)
            ul = upref[:, here].astype(F32) * long_out
            r.gr[start : start + 256, here] = (g_pre * s * long_out).astype(BF)
            r.dg[start : start + 256, here] = (ul * s * (1.0 + g_pre * (1.0 - s))).astype(BF)
        return carry

    def put_term(n, i, c, blk):
        axis, start, w, _ = PARTS[n]
        ref = getattr(r, f"p{n}")
        lo, at = i // 2, lax.rem(i, 2) * 2
        first, last = max(c, start), min(c + 256, start + w)
        blk = blk[:, first - c : last - c].astype(BF)
        span, width = pl.ds(first - start, last - first), last - first
        if axis == "x":
            ref[lo, pl.ds(at, 2), :, span] = blk.reshape(2, 256, width)
        elif axis == "y":
            ref[lo, pl.ds(at * 8, 16), :, :, span] = blk.reshape(16, 2, 16, width)
        else:
            ref[pl.ds(i * 4, 4), :, :, span] = blk.reshape(4, 4, 32, width)

    def terms(c, *parts):
        def step(i, carry):
            at = pl.ds(pl.multiple_of(i * 512, 512), 512)
            blk = dot(r.xt[at, :], r.dg[:, c : c + 256])
            for n in parts:
                put_term(n, i, c, blk)
            return carry

        lax.fori_loop(0, 4, step, 0)

    def share(axis, ref, lead, o):
        if axis == "y":
            t = lax.rem(y + o, 4)
            return ref.at[lax.rem(t, 2), :, t // 2]
        t = lax.rem((x if axis == "x" else z) + o, 4)
        return ref.at[t] if lead == 0 else ref.at[:, t]

    peer_of = dict(x=x_peer, y=y_peer, z=z_peer)

    def across(axis, ref, lead, dst):
        return [
            remote(share(axis, ref, lead, o), dst.at[o - 1], peer_of[axis](o)) for o in (1, 3, 2)
        ]

    flight = {}

    def halves(ref):
        half = ref.shape[0] // 2
        return ref.at[pl.ds(0, half)], ref.at[pl.ds(half, half)]

    def start_ring(n):
        axis = PARTS[n][0]
        if not PARTS[n][3]:
            start_stage(n, 0)
            return
        term, relay, got = (getattr(r, f"{c}{n}") for c in "pra")
        ahead, behind, far = (halves(share(axis, term, 1, o)) for o in (1, 3, 2))
        got_a, got_b = halves(got.at[0]), halves(got.at[1])
        up, down = peer_of[axis](1), peer_of[axis](3)
        relays = [remote(far[0], relay.at[0], up), remote(far[1], relay.at[1], down)]
        direct = [remote(ahead[1], got_a[1], up), remote(behind[0], got_b[0], down)]
        flight[n, "relay"] = relays
        flight[n, 0] = direct

    def pass_on(n):
        axis = PARTS[n][0]
        if not PARTS[n][3]:
            return
        term, relay, got = (getattr(r, f"{c}{n}") for c in "pra")
        ahead, behind = (halves(share(axis, term, 1, o)) for o in (1, 3))
        got_a, got_b = halves(got.at[0]), halves(got.at[1])
        up, down = peer_of[axis](1), peer_of[axis](3)
        for i, (held, dst, peer) in enumerate(((ahead[0], got_a[0], up), (behind[1], got_b[1], down))):
            flight[n, "relay"][i].wait_recv()
            held[...] = (held[...].astype(F32) + relay[i].astype(F32)).astype(BF)
            flight[n, 0].append(remote(held, dst, peer))

    def start_stage(n, stage):
        axis = ROUTES[PARTS[n][0]][0][stage]
        ref = getattr(r, f"{'pst'[stage]}{n}")
        lead = len(ref.shape) - 3 if stage == 2 else 1
        flight[n, stage] = across(axis, ref, lead, getattr(r, f"{'abc'[stage]}{n}"))

    def end_stage(n, stage):
        axis = ROUTES[PARTS[n][0]][0][stage]
        w = PARTS[n][2]
        for copy in flight[n, stage]:
            copy.wait_recv()
        ref = getattr(r, f"{'pst'[stage]}{n}")
        got = getattr(r, f"{'abc'[stage]}{n}")
        held = share(axis, ref, len(ref.shape) - 3 if stage == 2 else 1, 0)
        if stage == 0:
            out = getattr(r, f"s{n}")
            steps, rows = {"x": (2, 256), "y": (32, 16), "z": (16, 32)}[axis]
            batch = 256 // rows

            def step(b, carry):
                at = pl.ds(b * batch, batch)
                total = held[at].astype(F32)
                for o in range(got.shape[0]):
                    total = total + got[o, at].astype(F32)
                total = total.astype(BF)
                if axis == "x":
                    out[pl.ds(b, 1)] = total.reshape(1, 8, 2, 16, w)
                elif axis == "y":
                    out[pl.ds(b * 4, 4)] = total.reshape(4, 4, 16, w)
                else:
                    out[pl.ds(b, 1)] = total.reshape(1, 4, 64, w)
                return carry

            lax.fori_loop(0, 2, step, 0)
            return
        total = held[...].astype(F32)
        for o in range(3):
            total = total + got[o].astype(F32)
        if stage == 1:
            out = getattr(r, f"t{n}")
            out[...] = total.astype(BF).reshape(out.shape)
        else:
            c = PARTS[n][1]
            r.fin[:, :, c : c + w] = total.reshape(2, 16, w)

    rims_d = []
    for wave in range(2):
        half = pl.ds(512 * wave, 512)
        lax.fori_loop(2 * wave, 2 * wave + 2, gate_block, 0)
        df_at, dr_at = r.df.at[pl.ds(0, 256), half], r.dr.at[pl.ds(256, 256), half]
        rims_d.append(remote(df_at, r.df.at[pl.ds(256, 256), half], at_chip(prv, core)))
        rims_d.append(remote(dr_at, r.dr.at[pl.ds(0, 256), half], at_chip(nxt, core)))
    for wave in range(2):
        half = pl.ds(512 * wave, 512)
        span = slice(512 * wave, 512 * wave + 512)
        short_conv(272, 272, 0, 0, 240, wave)
        if wave == 0:
            lax.fori_loop(0, 8, transposed, 0)
            lax.fori_loop(0, 8, transposed_flip, 0)
            for k in range(2):
                arrived(halo_src, r.halo.at[k], 8 + k)
            for i in range(2):
                r.xf[0:16, 512 * i : 512 * i + 512] = r.halo[0, :, pl.ds(offs[i], 512)]
        back = pl.ds(512 * (1 - wave), 512)
        for k in range(2):
            src = hidden.at[0, :, pl.ds(0, 512)]
            arrived(src, r.xf.at[pl.ds(16 + 128 * k, 128), half], k * 2 + wave)
            arrived(src, r.xn.at[pl.ds(128 * k, 128), back], 4 + k * 2 + 1 - wave)
        lax.fori_loop(2 * wave, 2 * wave + 2, flip_next, 0)

        @pl.when(chip == 0)
        def _():
            r.xf[0:272, span] = jnp.zeros((272, 512), BF)

        @pl.when(chip == 1)
        def _():
            r.xf[0:16, span] = jnp.zeros((16, 512), BF)

        @pl.when(chip == 7)
        def _():
            r.xr[256:528, span] = jnp.zeros((272, 512), BF)

        @pl.when(chip == 6)
        def _():
            r.xr[512:528, span] = jnp.zeros((16, 512), BF)

        short_conv(0, 0, 240, 240, 272, wave)
        lax.fori_loop(4 * wave, 4 * wave + 4, long_conv, 0)
        for c in ((0, 256), (768, 512))[wave]:
            terms(c, *[n for n, (_, b, w, _) in enumerate(PARTS) if b < c + 256 and c < b + w])
            for n in {256: EARLY, 768: LATE[:1], 512: LATE[1:]}.get(c, ()):
                start_ring(n)
    for n in EARLY:
        pass_on(n)

    def mix(i, carry):
        here = pl.ds(pl.multiple_of(i * 256, 256), 256)
        there = pl.ds(pl.multiple_of(768 - i * 256, 256), 256)
        rev = dot(r.gr[256:512, there], r.jm[...])
        r.mx[:, here] = (r.gr[0:256, here].astype(F32) + rev).astype(BF)
        return carry

    lax.fori_loop(0, 4, mix, 0)
    tail_local, tail_remote = [], []
    for i in range(2):
        span = pl.ds(512 * i, 512)
        dst = mixed.at[0, :, pl.ds(offs[i], 512)]
        tail_local.append(local(r.mx.at[pl.ds(own, 128), span], dst))
        tail_remote.append(remote(r.mx.at[pl.ds(theirs, 128), span], dst, partner))

    sm_own = r.sm.at[0, z]

    def back_conv(wave, g, carry):
        row, spot = 4 * wave, pl.ds(pl.multiple_of((g - 4 * wave) * 128, 128), 128)
        here = pl.ds(pl.multiple_of(g * 128, 128), 128)
        ds_f = dot(r.uu[g], r.df[:, here]).astype(BF)
        r.dsf[0:256, here] = ds_f
        ds_r = dot(r.tt[g], r.dr[:, here]).astype(BF)
        r.dsr[16:272, here] = ds_r
        lag_f = dot_nt(r.df[0:256, here], r.sf[:, here])
        r.ls[0, g] = skew_sum(lag_f, True)
        lag_r = dot_nt(r.dr[256:512, here], r.sr[:, here])
        r.ls[1, g] = skew_sum(lag_r, True)
        fwd = r.xf[256:528, here].astype(F32)
        rev = r.xr[0:272, here].astype(F32)
        ds_f32, ds_r32 = ds_f.astype(F32), ds_r.astype(F32)
        for k in range(4):
            xk = fwd[16:272] if k == 0 else pltpu.roll(fwd, k, 0)[16:272]
            rk = rev[0:256] if k == 0 else pltpu.roll(rev, 272 - k, 0)[0:256]
            total = jnp.sum(ds_f32 * xk + ds_r32 * rk, axis=0, keepdims=True)
            sm_own[row + k : row + k + 1, spot] = total
        return carry

    def d_input(i, carry):
        here = pl.ds(pl.multiple_of(i * 256, 256), 256)
        both = dot_nt(r.dg[...], r.w[here, :])
        r.dh[:, here] = both[0:256]
        r.dv[:, here] = both[256:512].astype(BF)
        return carry

    def turn_back(i, carry):
        here = pl.ds(pl.multiple_of(i * 256, 256), 256)
        there = pl.ds(pl.multiple_of(1792 - i * 256, 256), 256)
        r.dh[:, here] = r.dh[:, here] + dot(r.dv[:, there], r.jm[...])
        return carry

    def rims_of(wave):
        span = slice(512 * wave, 512 * wave + 512)
        for copy in rims_d[2 * wave : 2 * wave + 2]:
            copy.wait_recv()

        @pl.when(chip == 7)
        def _():
            r.df[256:512, span] = jnp.zeros((256, 512), BF)

        @pl.when(chip == 0)
        def _():
            r.dr[0:256, span] = jnp.zeros((256, 512), BF)

    def stages(parts, stage):
        for n in parts:
            end_stage(n, stage)
            start_stage(n, stage + 1)

    small_axes = ((z, z_peer), (y, y_peer), (x, x_peer))

    def small_send(stage):
        at, peer = small_axes[stage]
        return [remote(r.sm.at[stage, at], r.sm.at[stage, at], peer(o)) for o in (1, 3, 2)]

    def small_sum(stage, copies):
        for copy in copies:
            copy.wait_recv()
        return (r.sm[stage, 0] + r.sm[stage, 1]) + (r.sm[stage, 2] + r.sm[stage, 3])

    rims_of(0)
    lax.fori_loop(0, 4, lambda g, carry: back_conv(0, g, carry), 0)
    lax.fori_loop(0, 4, d_input, 0)
    for n in LATE:
        pass_on(n)
    rims_of(1)
    lax.fori_loop(4, 8, lambda g, carry: back_conv(1, g, carry), 0)
    rim_dsf = remote(r.dsf.at[pl.ds(0, 16)], r.dsf.at[pl.ds(256, 16)], at_chip(prv, core))
    rim_dsr = remote(r.dsr.at[pl.ds(256, 16)], r.dsr.at[pl.ds(0, 16)], at_chip(nxt, core))

    sums = []
    for strand in range(2):
        total = r.ls[strand, :, 0, :]
        for t in range(1, 8):
            total = total + pltpu.roll(r.ls[strand, :, t, :], 512 - t, 1)
        sums.append(total)
    lag_m = lax.broadcasted_iota(jnp.int32, (512, 256), 0)
    lag_k = lax.broadcasted_iota(jnp.int32, (512, 256), 1)
    turned = jnp.dot(
        sums[0],
        jnp.where(lag_m + lag_k == 256, 1.0, 0.0),
        precision=lax.Precision.HIGHEST,
        preferred_element_type=F32,
    )
    sm_own[:, 512:SMALL] = turned + sums[1][:, 0:256]
    small_0 = small_send(0)
    stages(EARLY, 0)
    stages(LATE, 0)
    lax.fori_loop(4, 6, d_input, 0)
    r.sm[1, y] = small_sum(0, small_0)
    small_1 = small_send(1)
    stages(EARLY, 1)
    lax.fori_loop(6, 8, d_input, 0)
    r.sm[2, x] = small_sum(1, small_1)
    small_2 = small_send(2)
    stages(LATE, 1)
    lax.fori_loop(0, 8, turn_back, 0)

    rim_dsf.wait_recv()
    rim_dsr.wait_recv()

    @pl.when(chip == 7)
    def _():
        r.dsf[256:272, :] = jnp.zeros((16, 1024), BF)

    @pl.when(chip == 0)
    def _():
        r.dsr[0:16, :] = jnp.zeros((16, 1024), BF)

    def short_back(g, carry):
        here = pl.ds(pl.multiple_of(g * 128, 128), 128)
        there = pl.ds(col(g, 128), 128)
        fwd = r.dsf[:, here].astype(F32)
        rev = r.dsr[:, here].astype(F32)
        acc_f = r.st[0:1, there] * fwd[0:256]
        acc_r = r.st[0:1, there] * rev[16:272]
        for k in range(1, 4):
            tap = r.st[k : k + 1, there]
            acc_f += tap * pltpu.roll(fwd, 272 - k, 0)[0:256]
            acc_r += tap * pltpu.roll(rev, k, 0)[16:272]
        r.dh[:, there] = r.dh[:, there] + acc_f
        r.dxr[:, here] = acc_r.astype(BF)
        return carry

    lax.fori_loop(0, 8, short_back, 0)
    for i in range(4):
        there = pl.ds(col(i, 256), 256)
        r.dh[:, there] = r.dh[:, there] + dot(r.dxr[:, 768 - 256 * i : 1024 - 256 * i], r.jm[...])
    r.dhs[...] = r.dh[pl.ds(theirs, 128), :].astype(BF)
    pair_d = remote(r.dhs, r.dhr, partner)

    pair_d.wait_recv()
    r.dho[...] = (r.dh[pl.ds(own, 128), :] + r.dhr[...].astype(F32)).astype(BF)
    tail_local.append(local(r.dho, dhid.at[0]))
    for n in range(len(PARTS)):
        end_stage(n, 2)
    for i in range(2):
        span = pl.ds(512 * i, 512)
        dst = ggate.at[:, pl.ds(offs[i], 512)]
        tail_local.append(local(r.fin.at[core, :, span], dst))
        tail_remote.append(remote(r.fin.at[other, :, span], dst, partner))

    r.smo[...] = small_sum(2, small_2)
    tail_local.append(local(r.smo, small.at[core]))
    tail_remote.append(remote(r.smo, small.at[core], partner))

    for copy in tail_local:
        copy.wait()
    for copy in tail_remote:
        copy.wait_recv()
    for copy in started:
        copy.wait_send()


def finish(mixed, ggate, small, dhid, mixed_out, ggate_out, dhid_out, short_out, long_out, *rest):
    sems = rest[-1]
    held = rest[:3]
    reads = [
        pltpu.make_async_copy(src, dst, sems.at[i])
        for i, (src, dst) in enumerate(zip((mixed, dhid, ggate), held))
    ]
    writes = [
        pltpu.make_async_copy(src, dst, sems.at[3 + i])
        for i, (src, dst) in enumerate(zip(held, (mixed_out, dhid_out, ggate_out)))
    ]
    small_v = rest[3]
    read_small = pltpu.make_async_copy(small, small_v, sems.at[6])
    read_small.start()
    for copy in reads:
        copy.start()
    read_small.wait()
    small = small_v
    for i, (half, row) in enumerate(((1, 0), (0, 0), (0, 4), (1, 4))):
        short_out[:, 512 * i : 512 * i + 512] = small[half, row : row + 4, 0:512]
    long_out[0:4, :] = small[1, 0:4, 512:SMALL]
    long_out[4:12, :] = small[0, :, 512:SMALL]
    long_out[12:16, :] = small[1, 4:8, 512:SMALL]
    for read, write in zip(reads, writes):
        read.wait()
        write.start()
    for write in writes:
        write.wait()


def body(hidden, short_taps, long_taps, gate_weight, upstream):
    outside = pl.BlockSpec(memory_space=pl.ANY)
    inside = pl.BlockSpec(memory_space=pltpu.VMEM)
    block = jax.ShapeDtypeStruct((1, 128, 2048), BF)
    gate_rows = jax.ShapeDtypeStruct((16, 2048), F32)
    mixed, ggate, small, dhid = pl.pallas_call(
        kernel,
        out_shape=(block, gate_rows, jax.ShapeDtypeStruct((2, 8, SMALL), F32), block),
        in_specs=[outside, inside, inside, outside, outside],
        out_specs=(outside,) * 4,
        scratch_shapes=[pltpu.VMEM(shape, dtype) for shape, dtype in SCRATCH.values()]
        + [
            pltpu.SemaphoreType.DMA((LOCAL_SEMS,)),
            pltpu.SemaphoreType.DMA((REMOTE_SEMS,)),
            pltpu.SemaphoreType.DMA((REMOTE_SEMS + 10,)),
        ],
        compiler_params=pltpu.CompilerParams(
            collective_id=0, has_side_effects=True, vmem_limit_bytes=60 * 1024 * 1024
        ),
        cost_estimate=pl.CostEstimate(
            flops=8 * 10**9, bytes_accessed=12 * 2**20, transcendentals=2**20
        ),
    )(hidden, short_taps, jnp.transpose(long_taps), gate_weight, upstream)
    mixed, ggate, dhid, grad_short, grad_long = pl.pallas_call(
        finish,
        out_shape=(
            block,
            gate_rows,
            block,
            jax.ShapeDtypeStruct((4, 2048), F32),
            jax.ShapeDtypeStruct((16, 256), F32),
        ),
        in_specs=[outside] * 4,
        out_specs=(outside, outside, outside, inside, inside),
        scratch_shapes=[
            pltpu.VMEM((1, 128, 2048), BF),
            pltpu.VMEM((1, 128, 2048), BF),
            pltpu.VMEM((16, 2048), F32),
            pltpu.VMEM((2, 8, SMALL), F32),
            pltpu.SemaphoreType.DMA((7,)),
        ],
        compiler_params=pltpu.CompilerParams(vmem_limit_bytes=60 * 1024 * 1024),
    )(mixed, ggate, small, dhid)
    return (mixed, ggate, grad_short, jnp.transpose(grad_long), dhid)


def solution(mesh):
    placed = (P("dp", "seq", None), P(), P(), P(), P("dp", "seq", None))
    return jax.shard_map(
        body,
        mesh=mesh,
        in_specs=placed,
        out_specs=(P("dp", "seq", None), P(("seq", "dp"), None), P(), P(), P("dp", "seq", None)),
        check_vma=False,
    )
```

```python
import types

import jax
import jax.numpy as jnp
from jax import lax
from jax.experimental import pallas as pl
from jax.experimental.pallas import tpu as pltpu
from jax.sharding import PartitionSpec as P

BF = jnp.bfloat16
F32 = jnp.float32
MESH = pl.DeviceIdType.MESH
NT = (((1,), (1,)), ((), ()))

PARTS = (("z", 0, 256, True), ("z", 256, 256, True), ("y", 768, 256, True), ("x", 512, 256, True))
EARLY = (0, 1)
LATE = tuple(range(2, len(PARTS)))
ROUTES = dict(
    x=("xyz", (2, 4, 256), (2, 8, 2, 16), (2, 4, 16), (2, 256), (8, 16), (2, 16)),
    y=("yzx", (2, 32, 2, 16), (8, 4, 16), (4, 32), (32, 16), (8, 16), (32,)),
    z=("zxy", (16, 4, 32), (2, 4, 64), (2, 2, 2, 16), (16, 32), (2, 64), (2, 16)),
)
RING = 4
SMALL = 768

SCRATCH = dict(
    hh=((512, 2048), BF),
    w=((2048, 1024), BF),
    up=((256, 1024), BF),
    upj=((256, 1024), BF),
    halo=((2, 16, 2048), BF),
    st=((4, 2048), F32),
    xf=((528, 1024), BF),
    xr=((528, 1024), BF),
    xn=((256, 1024), BF),
    sf=((512, 1024), BF),
    sr=((512, 1024), BF),
    df=((512, 1024), BF),
    dr=((512, 1024), BF),
    gate=((512, 1024), F32),
    gr=((512, 1024), BF),
    mx=((256, 1024), BF),
    dg=((512, 1024), BF),
    tt=((8, 256, 512), BF),
    uu=((8, 256, 512), BF),
    tv=((16, 512), F32),
    uv=((16, 512), F32),
    jm=((256, 256), BF),
    im=((256, 256), BF),
    xt=((2048, 512), BF),
    fin=((2, 16, 1024), F32),
    dsf=((272, 1024), BF),
    dsr=((272, 1024), BF),
    ls=((2, 8, 8, 512), F32),
    sm=((3, 4, 8, SMALL), F32),
    smo=((8, SMALL), F32),
    dh=((256, 2048), F32),
    dv=((256, 2048), BF),
    dxr=((256, 1024), BF),
    dhs=((128, 2048), BF),
    dhr=((128, 2048), BF),
    dho=((128, 2048), BF),
)
for n, (axis, _, columns, ring) in enumerate(PARTS):
    _, *layouts = ROUTES[axis]
    for m, layout in enumerate(layouts):
        copies_ = () if m < 3 else (2,) if m == 3 and ring else (3,)
        SCRATCH[f"{'pstabc'[m]}{n}"] = (copies_ + layout + (columns,), BF)
    if ring:
        SCRATCH[f"r{n}"] = ((2, layouts[3][0] // 2) + layouts[3][1:] + (columns,), BF)
LOCAL_SEMS = 16
REMOTE_SEMS = 110


def dot(a, b):
    return jnp.dot(a, b, preferred_element_type=F32)


def dot_nt(a, b):
    return lax.dot_general(a, b, NT, preferred_element_type=F32)


def skew_sum(m, to_left):
    rows, lanes = m.shape
    while rows > 8:
        rows //= 2
        shift = lanes - rows if to_left else rows
        m = m[:rows] + pltpu.roll(m[rows:], shift, 1)
    return m


def kernel(hidden, staps, ltaps, weight, upstream, mixed, ggate, small, dhid, *scratch):
    r = types.SimpleNamespace(**dict(zip(SCRATCH, scratch)))
    loc, send, recv = scratch[len(SCRATCH) :]

    seq, dp = lax.axis_index("seq"), lax.axis_index("dp")
    core = lax.rem(seq, 2)
    chip = seq // 2
    x = lax.rem(chip, 4)
    y_lo = chip // 4
    y_hi = lax.rem(dp, 2)
    y = y_hi * 2 + y_lo
    z = dp // 2
    other = 1 - core

    def at_chip(c, k):
        return {"seq": c * 2 + k, "dp": dp}

    def x_peer(o):
        return {"seq": (y_lo * 4 + lax.rem(x + o, 4)) * 2 + core, "dp": dp}

    def y_peer(o):
        t = lax.rem(y + o, 4)
        return {
            "seq": (lax.rem(t, 2) * 4 + x) * 2 + core,
            "dp": z * 2 + t // 2,
        }

    def z_peer(o):
        return {"seq": seq, "dp": lax.rem(z + o, 4) * 2 + y_hi}

    partner = at_chip(chip, other)
    nxt, prv = lax.rem(chip + 1, 8), lax.rem(chip + 7, 8)
    far_chip = lax.rem(chip + 6 + 4 * core, 8)
    peers = [partner]
    peers += [at_chip(lax.rem(chip + o, 8), k) for o in (1, 7, 2, 6) for k in range(2)]
    peers += [f(o) for f in (x_peer, y_peer, z_peer) for o in (1, 2, 3)]

    offs = [pl.multiple_of(512 * other, 512), pl.multiple_of(1024 + 512 * core, 512)]
    offs_other = [pl.multiple_of(512 * core, 512), pl.multiple_of(1024 + 512 * other, 512)]
    own = pl.multiple_of(core * 128, 128)
    theirs = pl.multiple_of(other * 128, 128)

    def col(g, width):
        half = 512 // width
        c = jnp.where(g < half, 512 * other + g * width, 512 + 512 * core + g * width)
        return pl.multiple_of(c, width)

    started = []
    count = [0]

    def remote(src, dst, device, recv_index=None):
        i = count[0]
        count[0] += 1
        copy = pltpu.make_async_remote_copy(
            src_ref=src,
            dst_ref=dst,
            send_sem=send.at[i],
            recv_sem=recv.at[i if recv_index is None else recv_index],
            device_id=device,
            device_id_type=MESH,
        )
        copy.start()
        started.append(copy)
        return copy

    lcount = [0]

    def local(src, dst):
        copy = pltpu.make_async_copy(src, dst, loc.at[lcount[0]])
        lcount[0] += 1
        copy.start()
        return copy

    in_h = local(hidden.at[0], r.hh.at[pl.ds(own, 128)])
    in_u = [
        local(
            upstream.at[0, :, pl.ds(offs[i], 512)],
            r.up.at[pl.ds(own, 128), pl.ds(512 * i, 512)],
        )
        for i in range(2)
    ]
    in_w = [
        local(weight.at[:, pl.ds(offs[i], 512)], r.w.at[:, pl.ds(512 * i, 512)])
        for i in range(2)
    ]

    barrier = pltpu.get_barrier_semaphore()
    for peer in peers:
        pl.semaphore_signal(barrier, inc=1, device_id=peer, device_id_type=MESH)

    pl.semaphore_wait(barrier, len(peers))
    base = REMOTE_SEMS
    pair_h = remote(hidden.at[0], r.hh.at[pl.ds(own, 128)], partner)

    def send_rims(wave):
        for k in range(2):
            for i, span, there in ((wave, 16 + own, True), (1 - wave, own, False)):
                off = (512 * (1 - k), 1024 + 512 * k)[i]
                src = hidden.at[0, :, pl.ds(off, 512)]
                at = (pl.ds(pl.multiple_of(span, 16), 128), pl.ds(512 * i, 512))
                index = base + (0 if there else 4) + core * 2 + i
                if there:
                    remote(src, r.xf.at[at], at_chip(nxt, k), index)
                else:
                    remote(src, r.xn.at[at], at_chip(prv, k), index)

    send_rims(0)
    halo_src = hidden.at[0, pl.ds(pl.multiple_of(core * 112, 16), 16)]
    for k in range(2):
        remote(halo_src, r.halo.at[other], at_chip(far_chip, k), base + 8 + other)
    pair_u = [
        remote(
            upstream.at[0, :, pl.ds(offs_other[i], 512)],
            r.up.at[pl.ds(own, 128), pl.ds(512 * i, 512)],
            partner,
        )
        for i in range(2)
    ]

    def arrived(src, dst, i):
        pltpu.make_async_remote_copy(
            src_ref=src,
            dst_ref=dst,
            send_sem=send.at[0],
            recv_sem=recv.at[base + i],
            device_id=partner,
            device_id_type=MESH,
        ).wait_recv()

    rows_i = lax.broadcasted_iota(jnp.int32, (256, 256), 0)
    cols_i = lax.broadcasted_iota(jnp.int32, (256, 256), 1)
    r.jm[...] = jnp.where(rows_i + cols_i == 255, 1.0, 0.0).astype(BF)
    r.im[...] = jnp.where(rows_i == cols_i, 1.0, 0.0).astype(BF)
    r.st[...] = staps[...].astype(F32)

    tap_i = lax.broadcasted_iota(jnp.int32, (256, 512), 0)
    lag_i = lax.broadcasted_iota(jnp.int32, (256, 512), 1)
    taps = ltaps[...]
    r.tv[...] = dot(taps, jnp.where(tap_i + lag_i == 256, 1.0, 0.0).astype(BF))
    r.uv[...] = dot(taps, jnp.where(tap_i == lag_i, 1.0, 0.0).astype(BF))

    def toeplitz(g, carry):
        gg = col(g, 128) // 128
        for vec, out in ((r.tv, r.tt), (r.uv, r.uu)):
            first = pltpu.roll(
                jnp.broadcast_to(vec[pl.ds(gg, 1), :], (32, 512)), 0, 1, stride=1, stride_axis=0
            )
            for b in range(8):
                block = first if b == 0 else pltpu.roll(first, 32 * b, 1)
                out[g, 32 * b : 32 * b + 32, :] = block.astype(BF)
        return carry


    lax.fori_loop(0, 8, toeplitz, 0)
    in_h.wait()
    pair_h.wait_recv()

    def flip_rows(i, carry):
        here = pl.multiple_of(i * 256, 256)
        there = pl.multiple_of(1792 - i * 256, 256)
        r.hh[256:512, pl.ds(here, 256)] = dot(r.hh[0:256, pl.ds(there, 256)], r.jm[...]).astype(BF)
        return carry

    lax.fori_loop(0, 8, flip_rows, 0)

    for i in range(2):
        span = slice(512 * i, 512 * i + 512)
        r.xf[272:528, span] = r.hh[0:256, pl.ds(offs[i], 512)]
        r.xr[0:256, span] = r.hh[256:512, pl.ds(offs[i], 512)]

    send_rims(1)

    def short_conv(src_f, dst_f, src_r, dst_r, count_, wave):
        def step(g, carry):
            here = pl.ds(pl.multiple_of(g * 128, 128), 128)
            there = pl.ds(col(g, 128), 128)
            fwd = r.xf[src_f : src_f + count_ + 16, here].astype(F32)
            rev = r.xr[src_r : src_r + count_ + 16, here].astype(F32)
            acc_f = r.st[0:1, there] * fwd[16:]
            acc_r = r.st[0:1, there] * rev[:count_]
            for k in range(1, 4):
                tap = r.st[k : k + 1, there]
                acc_f += tap * pltpu.roll(fwd, k, 0)[16:]
                acc_r += tap * pltpu.roll(rev, count_ + 16 - k, 0)[:count_]
            r.sf[dst_f : dst_f + count_, here] = acc_f.astype(BF)
            r.sr[dst_r : dst_r + count_, here] = acc_r.astype(BF)
            return carry

        lax.fori_loop(4 * wave, 4 * wave + 4, step, 0)

    for copy in in_w + in_u:
        copy.wait()
    for copy in pair_u:
        copy.wait_recv()

    def gate_block(i, carry):
        here = pl.ds(pl.multiple_of(i * 256, 256), 256)
        there = pl.ds(pl.multiple_of(768 - i * 256, 256), 256)
        r.gate[:, here] = dot(r.hh[...], r.w[:, here])
        r.upj[:, here] = dot(r.up[:, there], r.jm[...]).astype(BF)

        def rows(b, carry):
            at = pl.multiple_of(b * 32, 32)
            gf = r.gate[pl.ds(at, 32), here]
            gb = r.gate[pl.ds(at + 256, 32), here]
            uf = r.up[pl.ds(at, 32), here].astype(F32)
            ub = r.upj[pl.ds(at, 32), here].astype(F32)
            r.df[pl.ds(at, 32), here] = (uf * gf * jax.nn.sigmoid(gf)).astype(BF)
            r.dr[pl.ds(at + 256, 32), here] = (ub * gb * jax.nn.sigmoid(gb)).astype(BF)
            return carry

        return lax.fori_loop(0, 8, rows, carry, unroll=4)

    def transposed(i, carry):
        here = pl.ds(pl.multiple_of(i * 256, 256), 256)
        r.xt[here, 0:256] = dot_nt(r.im[...], r.hh[0:256, here]).astype(BF)
        return carry

    def transposed_flip(i, carry):
        here = pl.ds(pl.multiple_of(i * 256, 256), 256)
        there = pl.ds(pl.multiple_of(1792 - i * 256, 256), 256)
        r.xt[here, 256:512] = dot(r.jm[...], r.xt[there, 0:256]).astype(BF)
        return carry

    def flip_next(i, carry):
        here = pl.ds(pl.multiple_of(i * 256, 256), 256)
        there = pl.ds(pl.multiple_of(768 - i * 256, 256), 256)
        r.xr[256:512, here] = dot(r.xn[:, there], r.jm[...]).astype(BF)
        far = r.halo[1, :, pl.ds(col(3 - i, 256), 256)]
        r.xr[512:528, here] = dot(far, r.jm[...]).astype(BF)
        return carry

    def long_conv(g, carry):
        here = pl.ds(pl.multiple_of(g * 128, 128), 128)
        for start, mat, inp, upref in ((0, r.tt, r.sf, r.up), (256, r.uu, r.sr, r.upj)):
            long_out = dot(mat[g], inp[:, here])
            g_pre = r.gate[start : start + 256, here]
            s = jax.nn.sigmoid(g_pre)
            ul = upref[:, here].astype(F32) * long_out
            r.gr[start : start + 256, here] = (g_pre * s * long_out).astype(BF)
            r.dg[start : start + 256, here] = (ul * s * (1.0 + g_pre * (1.0 - s))).astype(BF)
        return carry

    def put_term(n, i, c, blk):
        axis, start, w, _ = PARTS[n]
        ref = getattr(r, f"p{n}")
        lo, at = i // 2, lax.rem(i, 2) * 2
        first, last = max(c, start), min(c + 256, start + w)
        blk = blk[:, first - c : last - c].astype(BF)
        span, width = pl.ds(first - start, last - first), last - first
        if axis == "x":
            ref[lo, pl.ds(at, 2), :, span] = blk.reshape(2, 256, width)
        elif axis == "y":
            ref[lo, pl.ds(at * 8, 16), :, :, span] = blk.reshape(16, 2, 16, width)
        else:
            ref[pl.ds(i * 4, 4), :, :, span] = blk.reshape(4, 4, 32, width)

    def terms(c, *parts):
        def step(i, carry):
            at = pl.ds(pl.multiple_of(i * 512, 512), 512)
            blk = dot(r.xt[at, :], r.dg[:, c : c + 256])
            for n in parts:
                put_term(n, i, c, blk)
            return carry

        lax.fori_loop(0, 4, step, 0)

    def share(axis, ref, lead, o):
        if axis == "y":
            t = lax.rem(y + o, 4)
            return ref.at[lax.rem(t, 2), :, t // 2]
        t = lax.rem((x if axis == "x" else z) + o, 4)
        return ref.at[t] if lead == 0 else ref.at[:, t]

    peer_of = dict(x=x_peer, y=y_peer, z=z_peer)

    def across(axis, ref, lead, dst):
        return [
            remote(share(axis, ref, lead, o), dst.at[o - 1], peer_of[axis](o)) for o in (1, 3, 2)
        ]

    flight = {}

    def halves(ref):
        half = ref.shape[0] // 2
        return ref.at[pl.ds(0, half)], ref.at[pl.ds(half, half)]

    def start_ring(n):
        axis = PARTS[n][0]
        if not PARTS[n][3]:
            start_stage(n, 0)
            return
        term, relay, got = (getattr(r, f"{c}{n}") for c in "pra")
        ahead, behind, far = (halves(share(axis, term, 1, o)) for o in (1, 3, 2))
        got_a, got_b = halves(got.at[0]), halves(got.at[1])
        up, down = peer_of[axis](1), peer_of[axis](3)
        relays = [remote(far[0], relay.at[0], up), remote(far[1], relay.at[1], down)]
        direct = [remote(ahead[1], got_a[1], up), remote(behind[0], got_b[0], down)]
        flight[n, "relay"] = relays
        flight[n, 0] = direct

    def pass_on(n):
        axis = PARTS[n][0]
        if not PARTS[n][3]:
            return
        term, relay, got = (getattr(r, f"{c}{n}") for c in "pra")
        ahead, behind = (halves(share(axis, term, 1, o)) for o in (1, 3))
        got_a, got_b = halves(got.at[0]), halves(got.at[1])
        up, down = peer_of[axis](1), peer_of[axis](3)
        for i, (held, dst, peer) in enumerate(((ahead[0], got_a[0], up), (behind[1], got_b[1], down))):
            flight[n, "relay"][i].wait_recv()
            held[...] = (held[...].astype(F32) + relay[i].astype(F32)).astype(BF)
            flight[n, 0].append(remote(held, dst, peer))

    def start_stage(n, stage):
        axis = ROUTES[PARTS[n][0]][0][stage]
        ref = getattr(r, f"{'pst'[stage]}{n}")
        lead = len(ref.shape) - 3 if stage == 2 else 1
        flight[n, stage] = across(axis, ref, lead, getattr(r, f"{'abc'[stage]}{n}"))

    def end_stage(n, stage):
        axis = ROUTES[PARTS[n][0]][0][stage]
        w = PARTS[n][2]
        for copy in flight[n, stage]:
            copy.wait_recv()
        ref = getattr(r, f"{'pst'[stage]}{n}")
        got = getattr(r, f"{'abc'[stage]}{n}")
        held = share(axis, ref, len(ref.shape) - 3 if stage == 2 else 1, 0)
        if stage == 0:
            out = getattr(r, f"s{n}")
            steps, rows = {"x": (2, 256), "y": (32, 16), "z": (16, 32)}[axis]
            batch = 256 // rows

            def step(b, carry):
                at = pl.ds(b * batch, batch)
                total = held[at].astype(F32)
                for o in range(got.shape[0]):
                    total = total + got[o, at].astype(F32)
                total = total.astype(BF)
                if axis == "x":
                    out[pl.ds(b, 1)] = total.reshape(1, 8, 2, 16, w)
                elif axis == "y":
                    out[pl.ds(b * 4, 4)] = total.reshape(4, 4, 16, w)
                else:
                    out[pl.ds(b, 1)] = total.reshape(1, 4, 64, w)
                return carry

            lax.fori_loop(0, 2, step, 0)
            return
        total = held[...].astype(F32)
        for o in range(3):
            total = total + got[o].astype(F32)
        if stage == 1:
            out = getattr(r, f"t{n}")
            out[...] = total.astype(BF).reshape(out.shape)
        else:
            c = PARTS[n][1]
            r.fin[:, :, c : c + w] = total.reshape(2, 16, w)

    rims_d = []
    for wave in range(2):
        half = pl.ds(512 * wave, 512)
        lax.fori_loop(2 * wave, 2 * wave + 2, gate_block, 0)
        df_at, dr_at = r.df.at[pl.ds(0, 256), half], r.dr.at[pl.ds(256, 256), half]
        rims_d.append(remote(df_at, r.df.at[pl.ds(256, 256), half], at_chip(prv, core)))
        rims_d.append(remote(dr_at, r.dr.at[pl.ds(0, 256), half], at_chip(nxt, core)))
    for wave in range(2):
        half = pl.ds(512 * wave, 512)
        span = slice(512 * wave, 512 * wave + 512)
        short_conv(272, 272, 0, 0, 240, wave)
        if wave == 0:
            lax.fori_loop(0, 8, transposed, 0)
            lax.fori_loop(0, 8, transposed_flip, 0)
            for k in range(2):
                arrived(halo_src, r.halo.at[k], 8 + k)
            for i in range(2):
                r.xf[0:16, 512 * i : 512 * i + 512] = r.halo[0, :, pl.ds(offs[i], 512)]
        back = pl.ds(512 * (1 - wave), 512)
        for k in range(2):
            src = hidden.at[0, :, pl.ds(0, 512)]
            arrived(src, r.xf.at[pl.ds(16 + 128 * k, 128), half], k * 2 + wave)
            arrived(src, r.xn.at[pl.ds(128 * k, 128), back], 4 + k * 2 + 1 - wave)
        lax.fori_loop(2 * wave, 2 * wave + 2, flip_next, 0)

        @pl.when(chip == 0)
        def _():
            r.xf[0:272, span] = jnp.zeros((272, 512), BF)

        @pl.when(chip == 1)
        def _():
            r.xf[0:16, span] = jnp.zeros((16, 512), BF)

        @pl.when(chip == 7)
        def _():
            r.xr[256:528, span] = jnp.zeros((272, 512), BF)

        @pl.when(chip == 6)
        def _():
            r.xr[512:528, span] = jnp.zeros((16, 512), BF)

        short_conv(0, 0, 240, 240, 272, wave)
        lax.fori_loop(4 * wave, 4 * wave + 4, long_conv, 0)
        for c in ((0, 256), (768, 512))[wave]:
            terms(c, *[n for n, (_, b, w, _) in enumerate(PARTS) if b < c + 256 and c < b + w])
            for n in {0: EARLY[:1], 256: EARLY[1:], 768: LATE[:1], 512: LATE[1:]}.get(c, ()):
                start_ring(n)
    for n in EARLY:
        pass_on(n)

    def mix(i, carry):
        here = pl.ds(pl.multiple_of(i * 256, 256), 256)
        there = pl.ds(pl.multiple_of(768 - i * 256, 256), 256)
        rev = dot(r.gr[256:512, there], r.jm[...])
        r.mx[:, here] = (r.gr[0:256, here].astype(F32) + rev).astype(BF)
        return carry

    lax.fori_loop(0, 4, mix, 0)
    tail_local, tail_remote = [], []
    for i in range(2):
        span = pl.ds(512 * i, 512)
        dst = mixed.at[0, :, pl.ds(offs[i], 512)]
        tail_local.append(local(r.mx.at[pl.ds(own, 128), span], dst))
        tail_remote.append(remote(r.mx.at[pl.ds(theirs, 128), span], dst, partner))

    sm_own = r.sm.at[0, z]

    def back_conv(wave, g, carry):
        row, spot = 4 * wave, pl.ds(pl.multiple_of((g - 4 * wave) * 128, 128), 128)
        here = pl.ds(pl.multiple_of(g * 128, 128), 128)
        ds_f = dot(r.uu[g], r.df[:, here]).astype(BF)
        r.dsf[0:256, here] = ds_f
        ds_r = dot(r.tt[g], r.dr[:, here]).astype(BF)
        r.dsr[16:272, here] = ds_r
        lag_f = dot_nt(r.df[0:256, here], r.sf[:, here])
        r.ls[0, g] = skew_sum(lag_f, True)
        lag_r = dot_nt(r.dr[256:512, here], r.sr[:, here])
        r.ls[1, g] = skew_sum(lag_r, True)
        fwd = r.xf[256:528, here].astype(F32)
        rev = r.xr[0:272, here].astype(F32)
        ds_f32, ds_r32 = ds_f.astype(F32), ds_r.astype(F32)
        for k in range(4):
            xk = fwd[16:272] if k == 0 else pltpu.roll(fwd, k, 0)[16:272]
            rk = rev[0:256] if k == 0 else pltpu.roll(rev, 272 - k, 0)[0:256]
            total = jnp.sum(ds_f32 * xk + ds_r32 * rk, axis=0, keepdims=True)
            sm_own[row + k : row + k + 1, spot] = total
        return carry

    def d_input(i, carry):
        here = pl.ds(pl.multiple_of(i * 256, 256), 256)
        both = dot_nt(r.dg[...], r.w[here, :])
        r.dh[:, here] = both[0:256]
        r.dv[:, here] = both[256:512].astype(BF)
        return carry

    def turn_back(i, carry):
        here = pl.ds(pl.multiple_of(i * 256, 256), 256)
        there = pl.ds(pl.multiple_of(1792 - i * 256, 256), 256)
        r.dh[:, here] = r.dh[:, here] + dot(r.dv[:, there], r.jm[...])
        return carry

    def rims_of(wave):
        span = slice(512 * wave, 512 * wave + 512)
        for copy in rims_d[2 * wave : 2 * wave + 2]:
            copy.wait_recv()

        @pl.when(chip == 7)
        def _():
            r.df[256:512, span] = jnp.zeros((256, 512), BF)

        @pl.when(chip == 0)
        def _():
            r.dr[0:256, span] = jnp.zeros((256, 512), BF)

    def stages(parts, stage):
        for n in parts:
            end_stage(n, stage)
            start_stage(n, stage + 1)

    small_axes = ((z, z_peer), (y, y_peer), (x, x_peer))

    def small_send(stage):
        at, peer = small_axes[stage]
        return [remote(r.sm.at[stage, at], r.sm.at[stage, at], peer(o)) for o in (1, 3, 2)]

    def small_sum(stage, copies):
        for copy in copies:
            copy.wait_recv()
        return (r.sm[stage, 0] + r.sm[stage, 1]) + (r.sm[stage, 2] + r.sm[stage, 3])

    rims_of(0)
    lax.fori_loop(0, 4, lambda g, carry: back_conv(0, g, carry), 0)
    lax.fori_loop(0, 4, d_input, 0)
    for n in LATE:
        pass_on(n)
    rims_of(1)
    lax.fori_loop(4, 8, lambda g, carry: back_conv(1, g, carry), 0)
    rim_dsf = remote(r.dsf.at[pl.ds(0, 16)], r.dsf.at[pl.ds(256, 16)], at_chip(prv, core))
    rim_dsr = remote(r.dsr.at[pl.ds(256, 16)], r.dsr.at[pl.ds(0, 16)], at_chip(nxt, core))

    sums = []
    for strand in range(2):
        total = r.ls[strand, :, 0, :]
        for t in range(1, 8):
            total = total + pltpu.roll(r.ls[strand, :, t, :], 512 - t, 1)
        sums.append(total)
    lag_m = lax.broadcasted_iota(jnp.int32, (512, 256), 0)
    lag_k = lax.broadcasted_iota(jnp.int32, (512, 256), 1)
    turned = jnp.dot(
        sums[0],
        jnp.where(lag_m + lag_k == 256, 1.0, 0.0),
        precision=lax.Precision.HIGHEST,
        preferred_element_type=F32,
    )
    sm_own[:, 512:SMALL] = turned + sums[1][:, 0:256]
    small_0 = small_send(0)
    stages(EARLY, 0)
    stages(LATE, 0)
    lax.fori_loop(4, 6, d_input, 0)
    r.sm[1, y] = small_sum(0, small_0)
    small_1 = small_send(1)
    stages(EARLY, 1)
    lax.fori_loop(6, 8, d_input, 0)
    r.sm[2, x] = small_sum(1, small_1)
    small_2 = small_send(2)
    stages(LATE, 1)
    lax.fori_loop(0, 8, turn_back, 0)

    rim_dsf.wait_recv()
    rim_dsr.wait_recv()

    @pl.when(chip == 7)
    def _():
        r.dsf[256:272, :] = jnp.zeros((16, 1024), BF)

    @pl.when(chip == 0)
    def _():
        r.dsr[0:16, :] = jnp.zeros((16, 1024), BF)

    def short_back(g, carry):
        here = pl.ds(pl.multiple_of(g * 128, 128), 128)
        there = pl.ds(col(g, 128), 128)
        fwd = r.dsf[:, here].astype(F32)
        rev = r.dsr[:, here].astype(F32)
        acc_f = r.st[0:1, there] * fwd[0:256]
        acc_r = r.st[0:1, there] * rev[16:272]
        for k in range(1, 4):
            tap = r.st[k : k + 1, there]
            acc_f += tap * pltpu.roll(fwd, 272 - k, 0)[0:256]
            acc_r += tap * pltpu.roll(rev, k, 0)[16:272]
        r.dh[:, there] = r.dh[:, there] + acc_f
        r.dxr[:, here] = acc_r.astype(BF)
        return carry

    lax.fori_loop(0, 8, short_back, 0)
    for i in range(4):
        there = pl.ds(col(i, 256), 256)
        r.dh[:, there] = r.dh[:, there] + dot(r.dxr[:, 768 - 256 * i : 1024 - 256 * i], r.jm[...])
    r.dhs[...] = r.dh[pl.ds(theirs, 128), :].astype(BF)
    pair_d = remote(r.dhs, r.dhr, partner)

    pair_d.wait_recv()
    r.dho[...] = (r.dh[pl.ds(own, 128), :] + r.dhr[...].astype(F32)).astype(BF)
    tail_local.append(local(r.dho, dhid.at[0]))
    for n in range(len(PARTS)):
        end_stage(n, 2)
    for i in range(2):
        span = pl.ds(512 * i, 512)
        dst = ggate.at[:, pl.ds(offs[i], 512)]
        tail_local.append(local(r.fin.at[core, :, span], dst))
        tail_remote.append(remote(r.fin.at[other, :, span], dst, partner))

    r.smo[...] = small_sum(2, small_2)
    tail_local.append(local(r.smo, small.at[core]))
    tail_remote.append(remote(r.smo, small.at[core], partner))

    for copy in tail_local:
        copy.wait()
    for copy in tail_remote:
        copy.wait_recv()
    for copy in started:
        copy.wait_send()


def finish(mixed, ggate, small, dhid, mixed_out, ggate_out, dhid_out, short_out, long_out, *rest):
    sems = rest[-1]
    held = rest[:3]
    reads = [
        pltpu.make_async_copy(src, dst, sems.at[i])
        for i, (src, dst) in enumerate(zip((mixed, dhid, ggate), held))
    ]
    writes = [
        pltpu.make_async_copy(src, dst, sems.at[3 + i])
        for i, (src, dst) in enumerate(zip(held, (mixed_out, dhid_out, ggate_out)))
    ]
    small_v = rest[3]
    read_small = pltpu.make_async_copy(small, small_v, sems.at[6])
    read_small.start()
    for copy in reads:
        copy.start()
    read_small.wait()
    small = small_v
    for i, (half, row) in enumerate(((1, 0), (0, 0), (0, 4), (1, 4))):
        short_out[:, 512 * i : 512 * i + 512] = small[half, row : row + 4, 0:512]
    long_out[0:4, :] = small[1, 0:4, 512:SMALL]
    long_out[4:12, :] = small[0, :, 512:SMALL]
    long_out[12:16, :] = small[1, 4:8, 512:SMALL]
    for read, write in zip(reads, writes):
        read.wait()
        write.start()
    for write in writes:
        write.wait()


def body(hidden, short_taps, long_taps, gate_weight, upstream):
    outside = pl.BlockSpec(memory_space=pl.ANY)
    inside = pl.BlockSpec(memory_space=pltpu.VMEM)
    block = jax.ShapeDtypeStruct((1, 128, 2048), BF)
    gate_rows = jax.ShapeDtypeStruct((16, 2048), F32)
    mixed, ggate, small, dhid = pl.pallas_call(
        kernel,
        out_shape=(block, gate_rows, jax.ShapeDtypeStruct((2, 8, SMALL), F32), block),
        in_specs=[outside, inside, inside, outside, outside],
        out_specs=(outside,) * 4,
        scratch_shapes=[pltpu.VMEM(shape, dtype) for shape, dtype in SCRATCH.values()]
        + [
            pltpu.SemaphoreType.DMA((LOCAL_SEMS,)),
            pltpu.SemaphoreType.DMA((REMOTE_SEMS,)),
            pltpu.SemaphoreType.DMA((REMOTE_SEMS + 10,)),
        ],
        compiler_params=pltpu.CompilerParams(
            collective_id=0, has_side_effects=True, vmem_limit_bytes=60 * 1024 * 1024
        ),
        cost_estimate=pl.CostEstimate(
            flops=8 * 10**9, bytes_accessed=12 * 2**20, transcendentals=2**20
        ),
    )(hidden, short_taps, jnp.transpose(long_taps), gate_weight, upstream)
    mixed, ggate, dhid, grad_short, grad_long = pl.pallas_call(
        finish,
        out_shape=(
            block,
            gate_rows,
            block,
            jax.ShapeDtypeStruct((4, 2048), F32),
            jax.ShapeDtypeStruct((16, 256), F32),
        ),
        in_specs=[outside] * 4,
        out_specs=(outside, outside, outside, inside, inside),
        scratch_shapes=[
            pltpu.VMEM((1, 128, 2048), BF),
            pltpu.VMEM((1, 128, 2048), BF),
            pltpu.VMEM((16, 2048), F32),
            pltpu.VMEM((2, 8, SMALL), F32),
            pltpu.SemaphoreType.DMA((7,)),
        ],
        compiler_params=pltpu.CompilerParams(vmem_limit_bytes=60 * 1024 * 1024),
    )(mixed, ggate, small, dhid)
    return (mixed, ggate, grad_short, jnp.transpose(grad_long), dhid)


def solution(mesh):
    placed = (P("dp", "seq", None), P(), P(), P(), P("dp", "seq", None))
    return jax.shard_map(
        body,
        mesh=mesh,
        in_specs=placed,
        out_specs=(P("dp", "seq", None), P(("seq", "dp"), None), P(), P(), P("dp", "seq", None)),
        check_vma=False,
    )
```
